32 devices in a mesh: pipe: 2 (over y), expert: 16 (over z, x, core).
Axes of the slice: x: 2, y: 2, z: 4, core: 2. Of those that a mesh axis runs over, the one named last changes fastest.
Arguments:
- forward_tokens: bfloat16 [2, 384, 3584], P('pipe', 'expert'), may hold values from -6 to 6
- forward_routing: int32 [2, 384, 1], P('pipe', 'expert'), may hold values from 0 to 1; in each aligned block of 24 rows (0 to 23, 24 to 47, ..., all dimensions but the last counted through in order) at most 12 rows name the same one
- forward_gates: float32 [2, 384], P('pipe', 'expert'), may hold values from 0.25 to 2.5
- backward_tokens: bfloat16 [2, 384, 3584], P('pipe', 'expert'), may hold values from -6 to 6
- backward_routing: int32 [2, 384, 1], P('pipe', 'expert'), may hold values from 0 to 1; in each aligned block of 24 rows (0 to 23, 24 to 47, ..., all dimensions but the last counted through in order) at most 12 rows name the same one
- backward_gates: float32 [2, 384], P('pipe', 'expert'), may hold values from 0.25 to 2.5
- cotangent: bfloat16 [2, 384, 3584], P('pipe', 'expert'), may hold values from -6 to 6
- gate_matrix: bfloat16 [2, 3584, 2048], P('pipe', None, 'expert'), as said below
- up_matrix: bfloat16 [2, 3584, 2048], P('pipe', None, 'expert'), as said below
- down_matrix: bfloat16 [2, 2048, 3584], P('pipe', 'expert'), as said below
Outputs:
- forward_output: bfloat16 [2, 384, 3584], P('pipe', 'expert')
- input_gradient: bfloat16 [2, 384, 3584], P('pipe', 'expert')
- gate_gradient: bfloat16 [2, 1792, 2048], P('pipe', None, 'expert')
- up_gradient: bfloat16 [2, 1792, 2048], P('pipe', None, 'expert')
- down_gradient: bfloat16 [2, 2048, 1792], P('pipe', 'expert')
The draws below stay inside these ranges and needn't reach their ends.
Inputs may be any that keep to these rules, and one draw needn't show every extreme that they name: `forward_routing`: in each device's 24 rows no expert is named more than 12 times. `backward_routing`: in each device's 24 rows no expert is named more than 12 times. `gate_matrix`: blocks p and 1 - p along the first dimension are equal. `up_matrix`: blocks p and 1 - p along the first dimension are equal. `down_matrix`: blocks p and 1 - p along the first dimension are equal.
All inputs are finite; a program needn't handle non-finite values.
Results may differ from the reference program's by a relative error of at most 0.0065.
Values may be sent and summed in bfloat16 or wider, within the bound.
A program may use at most 64 MiB of HBM per device.

```python
import math
import jax
import jax.numpy as jnp
import numpy as np
from jax import lax

MODEL_WIDTH = 3584
HID = 1024
SHARING_CARDS = 8
TOK = 24
EXPERTS = 2
HIDDEN_PER_CARD = 128
CAP = 12
N_PIPE = 2
N_EXPERT = 16


def mirrored(key, shape_half, factor):
    value_entries = jax.random.truncated_normal(key, -4.0, 4.0, shape_half, jnp.float32) * factor
    return jnp.concatenate([value_entries, value_entries[::-1]], axis=0)


def draw_gate_matrix(key, part):
    return mirrored(jax.random.fold_in(key, 11), (N_PIPE // 2, MODEL_WIDTH, N_EXPERT * HIDDEN_PER_CARD), MODEL_WIDTH ** (-0.5)).astype(jnp.bfloat16)


def draw_up_matrix(key, part):
    return mirrored(jax.random.fold_in(key, 23), (N_PIPE // 2, MODEL_WIDTH, N_EXPERT * HIDDEN_PER_CARD), MODEL_WIDTH ** (-0.5)).astype(jnp.bfloat16)


def draw_down_matrix(key, part):
    return mirrored(jax.random.fold_in(key, 37), (N_PIPE // 2, N_EXPERT * HIDDEN_PER_CARD, MODEL_WIDTH), HID ** (-0.5)).astype(jnp.bfloat16)


def level_of(stream_key, dims, shards, low, high):
    def one(axis_at, parts):
        steps = jax.random.uniform(jax.random.fold_in(jax.random.fold_in(stream_key, 6), axis_at), (parts,), jnp.float32, low / len(shards), high / len(shards))
        return jnp.repeat(jnp.exp(steps), dims[axis_at] // parts).reshape((-1,) + (1,) * (len(dims) - axis_at - 1))

    factor_of = one(*shards[0])
    for cut in shards[1:]:
        factor_of = factor_of * one(*cut)
    return factor_of


def deal_out(key, own, number, rows, number_of, top, bound, skew):
    sequence = jax.random.permutation(key, number_of)
    heavy_load, usual = portions_of(number_of, rows * top, bound, skew, True), portions_of(number_of, rows * top, bound, skew, False)
    places = jnp.arange(number_of)

    def named(tallies, rotation):
        used = int((tallies > 0).sum())
        fixed = max(1, used // 4)
        passed = fixed + (places - fixed + rotation * (used - fixed)) % max(1, number_of - fixed)
        return jnp.zeros((number_of,), jnp.int32).at[sequence[jnp.where(places < fixed, places, passed)]].set(jnp.asarray(tallies, jnp.int32))

    tallies = jnp.where(number % 4 == 0, named(heavy_load, number // 4), named(usual, number - number // 4 - 1))
    mixed = jax.random.permutation(jax.random.fold_in(own, 3), number_of)
    donor, sink = mixed[0:number_of // 2 * 2:2], mixed[1:number_of // 2 * 2:2]
    slack = jnp.minimum(tallies[donor] - 1, bound - tallies[sink]) // 2
    slack = jnp.where((donor == sequence[0]) | (sink == sequence[0]) | (tallies[sink] == 0), 0, jnp.maximum(slack, 0))
    passed = jax.random.randint(jax.random.fold_in(own, 4), (number_of // 2,), 0, 1 << 20) % (slack + 1)
    tallies = tallies.at[donor].add(-passed).at[sink].add(passed)
    labels = jnp.searchsorted(jnp.cumsum(tallies), jnp.arange(rows * top), side="right").astype(jnp.int32)
    listing = labels.reshape(top, rows).T
    listing = listing[jax.random.permutation(jax.random.fold_in(own, 1), rows)]
    rotation = jax.random.randint(jax.random.fold_in(own, 2), (rows, 1), 0, top)
    return jnp.take_along_axis(listing, (jnp.arange(top)[None, :] + rotation) % top, axis=1)


def portions_of(count, total, reach, slope, full):
    weights = [(1 << 20) // math.isqrt(grade ** slope) + 1 for grade in range(1, count + 1)]
    largest = reach if full else min(reach, max(-(-total // count), total * weights[0] // sum(weights)))
    least = 1 if total - largest >= count - 1 else 0
    given, surplus = [largest] + [least] * (count - 1), total - largest - least * (count - 1)
    while surplus > 0:
        free = [i for i in range(1, count) if given[i] < largest] or [i for i in range(1, count) if given[i] < reach]
        mass, budget = sum([weights[i] for i in free]), surplus
        for i in free:
            addition = min(reach - given[i], max(1, budget * weights[i] // mass), surplus)
            given[i] = given[i] + addition
            surplus = surplus - addition
    return np.array(given)


def centred(own_key, extent, width, bound, split=(), held_as=jnp.bfloat16):
    array = width * jax.random.normal(own_key, extent, jnp.float32)
    if split:
        array = array * level_of(own_key, extent, split, -0.22, 0.18)
    return jnp.clip(array, -bound, bound).astype(held_as)


def setup_inputs(seed: int = 0) -> dict:
    keys = jax.random.split(jax.random.key(seed), 11)
    forward_tokens = centred(keys[0], (N_PIPE, N_EXPERT * TOK, MODEL_WIDTH), 1.0, 6.0, ((0, 2), (1, 16)))
    forward_routing_keys = jax.random.split(jax.random.fold_in(keys[1], 1), N_PIPE * (N_EXPERT * TOK) // TOK)
    forward_routing_turns = jax.random.permutation(jax.random.fold_in(keys[1], 3), N_PIPE * (N_EXPERT * TOK) // TOK)
    forward_routing = jax.vmap(lambda own, number: deal_out(jax.random.fold_in(keys[1], 2), own, number, TOK, EXPERTS, 1, CAP, 2))(forward_routing_keys, forward_routing_turns).reshape((N_PIPE, N_EXPERT * TOK, 1))
    forward_gates = jnp.clip(jnp.exp(math.log(2.5) - 2.3025851 * jax.random.uniform(keys[2], (N_PIPE, N_EXPERT * TOK), jnp.float32) ** level_of(keys[2], (N_PIPE, N_EXPERT * TOK), ((0, 2), (1, 16)), -0.2, 0.2)), 0.25, 2.5)
    backward_tokens = centred(keys[3], (N_PIPE, N_EXPERT * TOK, MODEL_WIDTH), 1.0, 6.0, ((0, 2), (1, 16)))
    backward_routing_keys = jax.random.split(jax.random.fold_in(keys[4], 1), N_PIPE * (N_EXPERT * TOK) // TOK)
    backward_routing_turns = jax.random.permutation(jax.random.fold_in(keys[4], 3), N_PIPE * (N_EXPERT * TOK) // TOK)
    backward_routing = jax.vmap(lambda own, number: deal_out(jax.random.fold_in(keys[4], 2), own, number, TOK, EXPERTS, 1, CAP, 2))(backward_routing_keys, backward_routing_turns).reshape((N_PIPE, N_EXPERT * TOK, 1))
    backward_gates = jnp.clip(jnp.exp(math.log(2.5) - 2.3025851 * jax.random.uniform(keys[5], (N_PIPE, N_EXPERT * TOK), jnp.float32) ** level_of(keys[5], (N_PIPE, N_EXPERT * TOK), ((0, 2), (1, 16)), -0.2, 0.2)), 0.25, 2.5)
    cotangent = centred(keys[6], (N_PIPE, N_EXPERT * TOK, MODEL_WIDTH), 1.0, 6.0, ((0, 2), (1, 16)))
    gate_matrix = draw_gate_matrix(jax.random.fold_in(keys[10], 71), 0)
    up_matrix = draw_up_matrix(jax.random.fold_in(keys[10], 71), 0)
    down_matrix = draw_down_matrix(jax.random.fold_in(keys[10], 71), 0)
    return {"forward_tokens": forward_tokens, "forward_routing": forward_routing, "forward_gates": forward_gates, "backward_tokens": backward_tokens, "backward_routing": backward_routing, "backward_gates": backward_gates, "cotangent": cotangent, "gate_matrix": gate_matrix, "up_matrix": up_matrix, "down_matrix": down_matrix}


def row_places(routing):
    sources = routing.reshape(N_EXPERT, TOK)
    members = (sources[:, :, None] == jnp.arange(EXPERTS, dtype=jnp.int32)[None, None, :]).astype(jnp.int32)
    earlier = jnp.cumsum(members, axis=1) - members
    within = jnp.sum(earlier * members, axis=2)
    anchors = jnp.arange(N_EXPERT, dtype=jnp.int32)[:, None]
    return (sources * (N_EXPERT * CAP) + anchors * CAP + within).reshape(-1).astype(jnp.int32)


def expert_rows(value_entries, places):
    zeroed = jnp.zeros((EXPERTS * N_EXPERT * CAP, MODEL_WIDTH), value_entries.dtype)
    return zeroed.at[places].set(value_entries).reshape(EXPERTS, N_EXPERT * CAP, MODEL_WIDTH)


def member_parts(left_section, right_section):
    return jnp.einsum("wey,eyk->wek", left_section.reshape(-1, SHARING_CARDS, HIDDEN_PER_CARD).astype(jnp.float32), right_section.reshape(SHARING_CARDS, HIDDEN_PER_CARD, MODEL_WIDTH).astype(jnp.float32))


def rounded_total(partials):
    rounded = lax.optimization_barrier(partials.astype(jnp.bfloat16))
    return jnp.sum(rounded.astype(jnp.float32), axis=1)


def expert_forward(item):
    rows, gate_block, up_block, down_block = item
    gate_pre = jnp.dot(rows, gate_block, preferred_element_type=jnp.float32)
    up_pre = jnp.dot(rows, up_block, preferred_element_type=jnp.float32)
    hidden = (jax.nn.silu(gate_pre) * up_pre).astype(jnp.bfloat16)
    return rounded_total(member_parts(hidden, down_block))


def expert_backward(item):
    rows, grads, gate_block, up_block, down_block = item
    gate_pre = jnp.dot(rows, gate_block, preferred_element_type=jnp.float32)
    up_pre = jnp.dot(rows, up_block, preferred_element_type=jnp.float32)
    sigma = jax.nn.sigmoid(gate_pre)
    activated = gate_pre * sigma
    hidden = (activated * up_pre).astype(jnp.bfloat16)
    hidden_grad = jnp.dot(grads, down_block.T, preferred_element_type=jnp.float32)
    gate_grad = (hidden_grad * up_pre * sigma * (1.0 + gate_pre * (1.0 - sigma))).astype(jnp.bfloat16)
    up_grad = (hidden_grad * activated).astype(jnp.bfloat16)
    summed = rounded_total(member_parts(gate_grad, gate_block.T) + member_parts(up_grad, up_block.T))
    gate_weight_grad = jnp.dot(rows.T, gate_grad, preferred_element_type=jnp.float32).astype(jnp.bfloat16)
    up_weight_grad = jnp.dot(rows.T, up_grad, preferred_element_type=jnp.float32).astype(jnp.bfloat16)
    down_weight_grad = jnp.dot(hidden.T, grads, preferred_element_type=jnp.float32).astype(jnp.bfloat16)
    return summed, gate_weight_grad, up_weight_grad, down_weight_grad


def position(forward_tokens, forward_routing, forward_gates, backward_tokens, backward_routing, backward_gates, cotangent, gate_matrix, up_matrix, down_matrix):
    gate_blocks = gate_matrix.reshape(MODEL_WIDTH, EXPERTS, HID).transpose(1, 0, 2)
    up_blocks = up_matrix.reshape(MODEL_WIDTH, EXPERTS, HID).transpose(1, 0, 2)
    down_blocks = down_matrix.reshape(EXPERTS, HID, MODEL_WIDTH)
    forward_places = row_places(forward_routing)
    forward_row_set = expert_rows(forward_tokens, forward_places)
    forward_sums = lax.map(expert_forward, (forward_row_set, gate_blocks, up_blocks, down_blocks)).reshape(-1, MODEL_WIDTH)
    forward_result = (forward_gates[:, None] * forward_sums[forward_places]).astype(jnp.bfloat16)
    scaled = (backward_gates[:, None] * cotangent.astype(jnp.float32)).astype(jnp.bfloat16)
    backward_places = row_places(backward_routing)
    backward_rows = expert_rows(backward_tokens, backward_places)
    scaled_rows = expert_rows(scaled, backward_places)
    backward_sums, gate_grads, up_grads, down_grads = lax.map(expert_backward, (backward_rows, scaled_rows, gate_blocks, up_blocks, down_blocks))
    backward_result = backward_sums.reshape(-1, MODEL_WIDTH)[backward_places].astype(jnp.bfloat16)
    gate_total = gate_grads.transpose(1, 0, 2).reshape(MODEL_WIDTH, EXPERTS * HID)
    up_total = up_grads.transpose(1, 0, 2).reshape(MODEL_WIDTH, EXPERTS * HID)
    down_total = down_grads.reshape(EXPERTS * HID, MODEL_WIDTH)
    return forward_result, backward_result, gate_total, up_total, down_total


def reference(forward_tokens, forward_routing, forward_gates, backward_tokens, backward_routing, backward_gates, cotangent, gate_matrix, up_matrix, down_matrix):
    middle = MODEL_WIDTH // 2

    def at_position(where):
        return position(forward_tokens[where], forward_routing[where, :, 0], forward_gates[where], backward_tokens[where], backward_routing[where, :, 0], backward_gates[where], cotangent[where], gate_matrix[where], up_matrix[where], down_matrix[where])

    def mirrored_pair(lower):
        upper = N_PIPE - 1 - lower
        first = at_position(lower)
        second = at_position(upper)
        first_grads = lax.optimization_barrier(first[2:])
        second_grads = lax.optimization_barrier(second[2:])
        totals = [(left_grad.astype(jnp.float32) + right_grad.astype(jnp.float32)).astype(jnp.bfloat16) for left_grad, right_grad in zip(first_grads, second_grads)]
        return (first[0], first[1], second[0], second[1], totals[0][:middle], totals[0][middle:], totals[1][:middle], totals[1][middle:], totals[2][:, :middle], totals[2][:, middle:])

    results = lax.map(mirrored_pair, jnp.arange(N_PIPE // 2, dtype=jnp.int32))

    def joined(lower_blocks, upper_blocks):
        return jnp.concatenate([lower_blocks, upper_blocks[::-1]], axis=0)

    return (joined(results[0], results[2]), joined(results[1], results[3]), joined(results[4], results[5]), joined(results[6], results[7]), joined(results[8], results[9]))
```

```python
import functools

import jax
import jax.numpy as jnp
from jax import lax
from jax.experimental import pallas as pl
from jax.experimental.pallas import tpu as pltpu
from jax.sharding import PartitionSpec as P

SHARING_CARDS = 8
PAD = 16
MESH = pl.DeviceIdType.MESH


def flip(value, bit):
    return value + bit - 2 * bit * ((value // bit) % 2)


def contract_last(left, right):
    return lax.dot_general(
        left, right, (((1,), (1,)), ((), ())), preferred_element_type=jnp.float32
    )


def matmul(left, right):
    return jnp.dot(left, right, preferred_element_type=jnp.float32)


def row_and_column(row):
    n = row.shape[1]
    at0 = lax.broadcasted_iota(jnp.int32, (n, n), 0)
    at1 = lax.broadcasted_iota(jnp.int32, (n, n), 1)
    return jnp.sum(jnp.where(at0 == at1, row, jnp.zeros_like(row)), axis=1, keepdims=True)


def places(routing_row):
    n = routing_row.shape[1]
    column = row_and_column(routing_row)
    at0 = lax.broadcasted_iota(jnp.int32, (n, n), 0)
    at1 = lax.broadcasted_iota(jnp.int32, (n, n), 1)
    same = column == routing_row
    before_row = jnp.sum(jnp.where(same & (at0 < at1), 1.0, 0.0), axis=0, keepdims=True)
    before_column = jnp.sum(jnp.where(same & (at1 < at0), 1.0, 0.0), axis=1, keepdims=True)
    return (
        routing_row * PAD + before_row.astype(jnp.int32),
        column * PAD + before_column.astype(jnp.int32),
    )


def kernel(
    experts,
    positions,
    ftok,
    froute,
    fgate,
    btok,
    broute,
    bgate,
    cot,
    wg,
    wu,
    wd,
    out_f,
    out_b,
    out_g,
    out_u,
    out_d,
    wgu,
    placed_b,
    placed_f,
    all_b,
    all_f,
    parts,
    r1,
    r2a,
    r2x,
    r2z,
    tsend,
    r3,
    pre,
    hgrad,
    grads,
    bhid,
    send_gu,
    send_d,
    recv_gu,
    recv_d,
    cross_s,
    cross_r,
    disp_s,
    disp_r,
    ret_s,
    ret_r,
    back_s,
    back_r,
    pipe_s,
    pipe_r,
):
    width = ftok.shape[1]
    hidden = wg.shape[1]
    middle = width // 2
    chunk = 512
    half_chunk = 256
    rows = 2 * 4 * experts * PAD
    e = lax.axis_index("expert")
    p = lax.axis_index("pipe")
    h = e // SHARING_CARDS
    m = e % SHARING_CARDS
    base = h * SHARING_CARDS
    c = m % 2
    o = 1 - c
    q = m // 2
    qx, qz = flip(q, 1), flip(q, 2)
    qd = flip(qx, 2)
    sib = {"expert": base + flip(m, 1)}
    xn = {"expert": base + flip(m, 2)}
    zn = {"expert": base + flip(m, 4)}
    mirror = {"pipe": positions - 1 - p}
    crosses = [{"expert": ((h + k) % experts) * SHARING_CARDS + m} for k in range(experts)]

    barrier = pltpu.get_barrier_semaphore()
    others = [sib, xn, zn, mirror] + crosses[1:]
    for other in others:
        pl.semaphore_signal(barrier, inc=1, device_id=other, device_id_type=MESH)

    def rc(src, dst, ss, rs, dev):
        return pltpu.make_async_remote_copy(
            src_ref=src, dst_ref=dst, send_sem=ss, recv_sem=rs, device_id=dev, device_id_type=MESH
        )

    sent = []

    def send(src, dst, ss, rs, dev):
        copy = rc(src, dst, ss, rs, dev)
        copy.start()
        sent.append(copy)

    bplace_row, bplace_col = places(broute[...])
    fplace_row, fplace_col = places(froute[...])
    at_place = lax.broadcasted_iota(jnp.int32, (experts * PAD, ftok.shape[0]), 0)
    bslots = jnp.where(at_place == bplace_row, 1.0, 0.0).astype(jnp.bfloat16)
    fslots_f32 = jnp.where(at_place == fplace_row, 1.0, 0.0)
    fslots = fslots_f32.astype(jnp.bfloat16)
    fgate_place = jnp.sum(fslots_f32 * fgate[...], axis=1, keepdims=True)
    scaled = (row_and_column(bgate[...]) * cot[...].astype(jnp.float32)).astype(jnp.bfloat16)
    placed_b[:, 0] = matmul(bslots, btok[...]).astype(jnp.bfloat16).reshape(experts, PAD, width)
    placed_b[:, 1] = matmul(bslots, scaled).astype(jnp.bfloat16).reshape(experts, PAD, width)
    placed_f[:, 0] = matmul(fslots, ftok[...]).astype(jnp.bfloat16).reshape(experts, PAD, width)
    all_b[c, q, h] = placed_b[h]
    all_f[c, q, h] = placed_f[h]

    pl.semaphore_wait(barrier, len(others))

    def origin(k):
        return (h + experts - k) % experts

    def cross_send(s, placed, alls):
        for k in range(1, experts):
            send(
                placed.at[(h + k) % experts],
                alls.at[c, q, h],
                cross_s.at[s, k],
                cross_r.at[s, k],
                crosses[k],
            )

    def spread(s, alls, k, kind, part, dev):
        slot = alls.at[part[0], part[1], origin(k)]
        send(slot, slot, disp_s.at[s, k, kind], disp_r.at[s, k, kind], dev)

    def arrive(s, alls, k, kind, part, dev):
        slot = alls.at[part[0], part[1], origin(k)]
        rc(slot, slot, disp_s.at[s, k, kind], disp_r.at[s, k, kind], dev).wait_recv()

    def direct(s, alls, k):
        if k > 0:
            slot = alls.at[c, q, origin(k)]
            rc(slot, slot, cross_s.at[s, k], cross_r.at[s, k], crosses[k]).wait_recv()
        spread(s, alls, k, 0, (c, q), xn)
        spread(s, alls, k, 1, (c, q), zn)
        spread(s, alls, k, 2, (c, q), sib)

    def forward(s, alls, k):
        arrive(s, alls, k, 0, (c, qx), xn)
        if k % 2 == 0:
            spread(s, alls, k, 5, (c, qx), zn)
        spread(s, alls, k, 3, (c, qx), sib)
        arrive(s, alls, k, 1, (c, qz), zn)
        if k % 2 == 1:
            spread(s, alls, k, 5, (c, qz), xn)
        spread(s, alls, k, 4, (c, qz), sib)

    def last(s, alls, k):
        arrive(s, alls, k, 5, (c, qd), zn if k % 2 == 0 else xn)
        spread(s, alls, k, 6, (c, qd), sib)

    def complete(s, alls, k):
        arrive(s, alls, k, 2, (o, q), sib)
        arrive(s, alls, k, 3, (o, qx), sib)
        arrive(s, alls, k, 4, (o, qz), sib)
        arrive(s, alls, k, 6, (o, qd), sib)

    cross_send(0, placed_b, all_b)
    direct(0, all_b, 0)
    cross_send(1, placed_f, all_f)
    direct(1, all_f, 0)
    wgu[:, :hidden] = wg[...]
    wgu[:, hidden:] = wu[...]
    forward(0, all_b, 0)
    last(0, all_b, 0)
    for k in range(1, experts):
        direct(0, all_b, k)
    forward(1, all_f, 0)
    last(1, all_f, 0)
    for k in range(1, experts):
        forward(0, all_b, k)
        direct(1, all_f, k)
    for k in range(1, experts):
        last(0, all_b, k)
    for k in range(experts):
        complete(0, all_b, k)

    def columns(i, size):
        return pl.ds(pl.multiple_of(i * size, size), size)

    pre[...] = jnp.zeros_like(pre)
    hgrad[...] = jnp.zeros_like(hgrad)

    def backward_step(i, carry):
        at = columns(i, chunk)
        y = all_b[:, :, :, 0, :, at].reshape(rows, chunk)
        g = all_b[:, :, :, 1, :, at].reshape(rows, chunk)
        pre[...] += matmul(y, wgu[at, :])
        hgrad[...] += contract_last(g, wd[:, at])
        return carry

    lax.fori_loop(0, width // chunk, backward_step, 0)
    gate_pre = pre[:, :hidden]
    up_pre = pre[:, hidden:]
    sigma = 1.0 / (1.0 + jnp.exp(-gate_pre))
    activated = gate_pre * sigma
    hidden_grad = hgrad[...]
    bhid[...] = (activated * up_pre).astype(jnp.bfloat16)
    grads[:, :hidden] = (
        hidden_grad * up_pre * sigma * (1.0 + gate_pre * (1.0 - sigma))
    ).astype(jnp.bfloat16)
    grads[:, hidden:] = (hidden_grad * activated).astype(jnp.bfloat16)

    for k in range(1, experts):
        forward(1, all_f, k)

    side = p // (positions // 2)
    own_start = side * middle
    other_start = (1 - side) * middle

    def weight_grads(start, gate_to, up_to, down_to):
        def step(i, carry):
            at = pl.ds(pl.multiple_of(start + i * half_chunk, half_chunk), half_chunk)
            to = pl.ds(pl.multiple_of(i * half_chunk, half_chunk), half_chunk)
            y = all_b[:, :, :, 0, :, at].reshape(rows, half_chunk)
            both = matmul(y.T, grads[...]).astype(jnp.bfloat16)
            gate_to[to, :] = both[:, :hidden]
            up_to[to, :] = both[:, hidden:]
            g = all_b[:, :, :, 1, :, at].reshape(rows, half_chunk)
            down_to[:, to] = matmul(bhid[...].T, g).astype(jnp.bfloat16)
            return carry

        lax.fori_loop(0, middle // half_chunk, step, 0)

    weight_grads(other_start, send_gu.at[0], send_gu.at[1], send_d)
    send(send_gu, recv_gu, pipe_s.at[0], pipe_r.at[0], mirror)
    send(send_d, recv_d, pipe_s.at[1], pipe_r.at[1], mirror)
    for k in range(1, experts):
        last(1, all_f, k)

    def back_step(i, carry):
        at = columns(i, chunk)
        value = contract_last(grads[...], wgu[at, :]).astype(jnp.bfloat16)
        parts[0, :, :, :, :, at] = value.reshape(2, 4, experts, PAD, chunk)
        return carry

    lax.fori_loop(0, width // chunk, back_step, 0)

    def to_sibling(s):
        send(parts.at[s, o], r1.at[s], ret_s.at[s, 0], ret_r.at[s, 0], sib)

    def pair_sum(s):
        rc(parts.at[s, o], r1.at[s], ret_s.at[s, 0], ret_r.at[s, 0], sib).wait_recv()

        def add(first):
            parts[s, c, first] = (
                parts[s, c, first].astype(jnp.float32) + r1[s, first].astype(jnp.float32)
            ).astype(jnp.bfloat16)

        add(qd)
        for j in range(experts):
            send(
                parts.at[s, c, qd, j],
                r2a.at[s, j],
                back_s.at[s, j, 0],
                back_r.at[s, j, 0],
                xn if j % 2 == 0 else zn,
            )
        add(qx)
        for j in range(0, experts, 2):
            send(
                parts.at[s, c, qx, j], r2x.at[s, j], back_s.at[s, j, 1], back_r.at[s, j, 1], xn
            )
        add(qz)
        for j in range(1, experts, 2):
            send(
                parts.at[s, c, qz, j], r2z.at[s, j], back_s.at[s, j, 2], back_r.at[s, j, 2], zn
            )
        add(q)

    def passed_on(s):
        for j in range(experts):
            even = j % 2 == 0
            rc(
                parts.at[s, c, qd, j],
                r2a.at[s, j],
                back_s.at[s, j, 0],
                back_r.at[s, j, 0],
                xn if even else zn,
            ).wait_recv()
            to = qz if even else qx
            parts[s, c, to, j] = (
                parts[s, c, to, j].astype(jnp.float32) + r2a[s, j].astype(jnp.float32)
            ).astype(jnp.bfloat16)
            if even:
                send(
                    parts.at[s, c, qz, j], r2z.at[s, j], back_s.at[s, j, 2], back_r.at[s, j, 2], zn
                )
            else:
                send(
                    parts.at[s, c, qx, j], r2x.at[s, j], back_s.at[s, j, 1], back_r.at[s, j, 1], xn
                )

    def summed(s):
        for j in range(experts):
            rc(
                parts.at[s, c, qx, j], r2x.at[s, j], back_s.at[s, j, 1], back_r.at[s, j, 1], xn
            ).wait_recv()
            rc(
                parts.at[s, c, qz, j], r2z.at[s, j], back_s.at[s, j, 2], back_r.at[s, j, 2], zn
            ).wait_recv()
            tsend[s, j] = (
                parts[s, c, q, j].astype(jnp.float32)
                + r2x[s, j].astype(jnp.float32)
                + r2z[s, j].astype(jnp.float32)
            ).astype(jnp.bfloat16)
        for k in range(1, experts):
            send(
                tsend.at[s, (h + k) % experts],
                r3.at[s, h],
                ret_s.at[s, k],
                ret_r.at[s, k],
                crosses[k],
            )
        r3[s, h] = tsend[s, h]

    def home(s):
        for k in range(1, experts):
            slot = r3.at[s, origin(k)]
            rc(slot, slot, ret_s.at[s, k], ret_r.at[s, k], crosses[k]).wait_recv()
        return r3[s].reshape(experts * PAD, width)

    to_sibling(0)

    for k in range(experts):
        complete(1, all_f, k)
    pre[...] = jnp.zeros_like(pre)

    def forward_step(i, carry):
        at = columns(i, chunk)
        x = all_f[:, :, :, 0, :, at].reshape(rows, chunk)
        pre[...] += matmul(x, wgu[at, :])
        return carry

    lax.fori_loop(0, width // chunk, forward_step, 0)
    fgate_pre = pre[:, :hidden]
    fhid = ((fgate_pre / (1.0 + jnp.exp(-fgate_pre))) * pre[:, hidden:]).astype(jnp.bfloat16)
    pair_sum(0)

    hgrad[...] = fhid.astype(jnp.float32)

    def parts_step(i, carry):
        at = columns(i, chunk)
        value = matmul(hgrad[...].astype(jnp.bfloat16), wd[:, at]).astype(jnp.bfloat16)
        parts[1, :, :, :, :, at] = value.reshape(2, 4, experts, PAD, chunk)
        return carry

    lax.fori_loop(0, width // chunk, parts_step, 0)
    to_sibling(1)
    passed_on(0)
    pair_sum(1)
    summed(0)
    passed_on(1)
    weight_grads(own_start, out_g, out_u, out_d)
    summed(1)

    at_place_t = lax.broadcasted_iota(jnp.int32, (ftok.shape[0], experts * PAD), 1)
    bslots_t = jnp.where(at_place_t == bplace_col, 1.0, 0.0).astype(jnp.bfloat16)
    fslots_t = jnp.where(at_place_t == fplace_col, 1.0, 0.0).astype(jnp.bfloat16)
    out_b[...] = matmul(bslots_t, home(0)).astype(jnp.bfloat16)
    gated = (fgate_place * home(1).astype(jnp.float32)).astype(jnp.bfloat16)
    out_f[...] = matmul(fslots_t, gated).astype(jnp.bfloat16)

    rc(send_gu, recv_gu, pipe_s.at[0], pipe_r.at[0], mirror).wait_recv()
    out_g[...] = (out_g[...].astype(jnp.float32) + recv_gu[0].astype(jnp.float32)).astype(
        jnp.bfloat16
    )
    out_u[...] = (out_u[...].astype(jnp.float32) + recv_gu[1].astype(jnp.float32)).astype(
        jnp.bfloat16
    )
    rc(send_d, recv_d, pipe_s.at[1], pipe_r.at[1], mirror).wait_recv()
    out_d[...] = (out_d[...].astype(jnp.float32) + recv_d[...].astype(jnp.float32)).astype(
        jnp.bfloat16
    )
    for copy in sent:
        copy.wait_send()


def on_device(
    forward_tokens,
    forward_routing,
    forward_gates,
    backward_tokens,
    backward_routing,
    backward_gates,
    cotangent,
    gate_matrix,
    up_matrix,
    down_matrix,
):
    devices = lax.axis_size("expert")
    positions = lax.axis_size("pipe")
    experts = devices // SHARING_CARDS
    tokens, width = forward_tokens.shape[1:]
    hidden = gate_matrix.shape[2]
    middle = width // 2
    rows = SHARING_CARDS * experts * PAD
    bf16, f32 = jnp.bfloat16, jnp.float32
    vmem = pl.BlockSpec(memory_space=pltpu.VMEM)
    dma = pltpu.SemaphoreType.DMA
    outs = pl.pallas_call(
        functools.partial(kernel, experts, positions),
        out_shape=(
            jax.ShapeDtypeStruct((tokens, width), bf16),
            jax.ShapeDtypeStruct((tokens, width), bf16),
            jax.ShapeDtypeStruct((middle, hidden), bf16),
            jax.ShapeDtypeStruct((middle, hidden), bf16),
            jax.ShapeDtypeStruct((hidden, middle), bf16),
        ),
        in_specs=[vmem] * 10,
        out_specs=(vmem,) * 5,
        scratch_shapes=[
            pltpu.VMEM((width, 2 * hidden), bf16),
            pltpu.VMEM((experts, 2, PAD, width), bf16),
            pltpu.VMEM((experts, 1, PAD, width), bf16),
            pltpu.VMEM((2, 4, experts, 2, PAD, width), bf16),
            pltpu.VMEM((2, 4, experts, 1, PAD, width), bf16),
            pltpu.VMEM((2, 2, 4, experts, PAD, width), bf16),
            pltpu.VMEM((2, 4, experts, PAD, width), bf16),
            pltpu.VMEM((2, experts, PAD, width), bf16),
            pltpu.VMEM((2, experts, PAD, width), bf16),
            pltpu.VMEM((2, experts, PAD, width), bf16),
            pltpu.VMEM((2, experts, PAD, width), bf16),
            pltpu.VMEM((2, experts, PAD, width), bf16),
            pltpu.VMEM((rows, 2 * hidden), f32),
            pltpu.VMEM((rows, hidden), f32),
            pltpu.VMEM((rows, 2 * hidden), bf16),
            pltpu.VMEM((rows, hidden), bf16),
            pltpu.VMEM((2, middle, hidden), bf16),
            pltpu.VMEM((hidden, middle), bf16),
            pltpu.VMEM((2, middle, hidden), bf16),
            pltpu.VMEM((hidden, middle), bf16),
            dma((2, experts)),
            dma((2, experts)),
            dma((2, experts, 7)),
            dma((2, experts, 7)),
            dma((2, experts)),
            dma((2, experts)),
            dma((2, experts, 3)),
            dma((2, experts, 3)),
            dma((2,)),
            dma((2,)),
        ],
        compiler_params=pltpu.CompilerParams(
            collective_id=0, has_side_effects=True, vmem_limit_bytes=56 * 1024 * 1024
        ),
    )(
        forward_tokens[0],
        forward_routing.reshape(1, tokens),
        forward_gates,
        backward_tokens[0],
        backward_routing.reshape(1, tokens),
        backward_gates,
        cotangent[0],
        gate_matrix[0],
        up_matrix[0],
        down_matrix[0],
    )
    return tuple(out[None] for out in outs)


def solution(mesh):
    in_specs = (
        P("pipe", "expert", None),
        P("pipe", "expert", None),
        P("pipe", "expert"),
        P("pipe", "expert", None),
        P("pipe", "expert", None),
        P("pipe", "expert"),
        P("pipe", "expert", None),
        P("pipe", None, "expert"),
        P("pipe", None, "expert"),
        P("pipe", "expert", None),
    )
    out_specs = (
        P("pipe", "expert", None),
        P("pipe", "expert", None),
        P("pipe", None, "expert"),
        P("pipe", None, "expert"),
        P("pipe", "expert", None),
    )
    return jax.shard_map(
        on_device, mesh=mesh, in_specs=in_specs, out_specs=out_specs, check_vma=False
    )
```

```python
import functools

import jax
import jax.numpy as jnp
from jax import lax
from jax.experimental import pallas as pl
from jax.experimental.pallas import tpu as pltpu
from jax.sharding import PartitionSpec as P

SHARING_CARDS = 8
PAD = 16
MESH = pl.DeviceIdType.MESH


def flip(value, bit):
    return value + bit - 2 * bit * ((value // bit) % 2)


def contract_last(left, right):
    return lax.dot_general(
        left, right, (((1,), (1,)), ((), ())), preferred_element_type=jnp.float32
    )


def matmul(left, right):
    return jnp.dot(left, right, preferred_element_type=jnp.float32)


def row_and_column(row):
    n = row.shape[1]
    at0 = lax.broadcasted_iota(jnp.int32, (n, n), 0)
    at1 = lax.broadcasted_iota(jnp.int32, (n, n), 1)
    return jnp.sum(jnp.where(at0 == at1, row, jnp.zeros_like(row)), axis=1, keepdims=True)


def places(routing_row):
    n = routing_row.shape[1]
    column = row_and_column(routing_row)
    at0 = lax.broadcasted_iota(jnp.int32, (n, n), 0)
    at1 = lax.broadcasted_iota(jnp.int32, (n, n), 1)
    same = column == routing_row
    before_row = jnp.sum(jnp.where(same & (at0 < at1), 1.0, 0.0), axis=0, keepdims=True)
    before_column = jnp.sum(jnp.where(same & (at1 < at0), 1.0, 0.0), axis=1, keepdims=True)
    return (
        routing_row * PAD + before_row.astype(jnp.int32),
        column * PAD + before_column.astype(jnp.int32),
    )


def kernel(
    experts,
    positions,
    ftok,
    froute,
    fgate,
    btok,
    broute,
    bgate,
    cot,
    wg,
    wu,
    wd,
    out_f,
    out_b,
    out_g,
    out_u,
    out_d,
    wgu,
    placed_b,
    placed_f,
    all_b,
    all_f,
    parts,
    r1,
    r2a,
    r2x,
    r2z,
    tsend,
    r3,
    pre,
    hgrad,
    grads,
    mgrads,
    mirrored,
    cross_s,
    cross_r,
    disp_s,
    disp_r,
    ret_s,
    ret_r,
    back_s,
    back_r,
    pipe_s,
    pipe_r,
    side_s,
    side_r,
):
    width = ftok.shape[1]
    hidden = wg.shape[1]
    middle = width // 2
    chunk = 512
    half_chunk = 256
    rows = 2 * 4 * experts * PAD
    e = lax.axis_index("expert")
    p = lax.axis_index("pipe")
    h = e // SHARING_CARDS
    m = e % SHARING_CARDS
    base = h * SHARING_CARDS
    c = m % 2
    o = 1 - c
    q = m // 2
    qx, qz = flip(q, 1), flip(q, 2)
    qd = flip(qx, 2)
    sib = {"expert": base + flip(m, 1)}
    xn = {"expert": base + flip(m, 2)}
    zn = {"expert": base + flip(m, 4)}
    mirror = {"pipe": positions - 1 - p}
    side = p // (positions // 2)
    other_half = pl.ds(pl.multiple_of((1 - side) * middle, middle), middle)
    crosses = [{"expert": ((h + k) % experts) * SHARING_CARDS + m} for k in range(experts)]

    barrier = pltpu.get_barrier_semaphore()
    others = [sib, xn, zn, mirror] + crosses[1:]
    for other in others:
        pl.semaphore_signal(barrier, inc=1, device_id=other, device_id_type=MESH)

    def rc(src, dst, ss, rs, dev):
        return pltpu.make_async_remote_copy(
            src_ref=src, dst_ref=dst, send_sem=ss, recv_sem=rs, device_id=dev, device_id_type=MESH
        )

    sent = []

    def send(src, dst, ss, rs, dev):
        copy = rc(src, dst, ss, rs, dev)
        copy.start()
        sent.append(copy)

    bplace_row, bplace_col = places(broute[...])
    fplace_row, fplace_col = places(froute[...])
    at_place = lax.broadcasted_iota(jnp.int32, (experts * PAD, ftok.shape[0]), 0)
    bslots = jnp.where(at_place == bplace_row, 1.0, 0.0).astype(jnp.bfloat16)
    fslots_f32 = jnp.where(at_place == fplace_row, 1.0, 0.0)
    fslots = fslots_f32.astype(jnp.bfloat16)
    fgate_place = jnp.sum(fslots_f32 * fgate[...], axis=1, keepdims=True)
    scaled = (row_and_column(bgate[...]) * cot[...].astype(jnp.float32)).astype(jnp.bfloat16)
    placed_b[:, 0] = matmul(bslots, btok[...]).astype(jnp.bfloat16).reshape(experts, PAD, width)
    placed_b[:, 1] = matmul(bslots, scaled).astype(jnp.bfloat16).reshape(experts, PAD, width)
    placed_f[:, 0] = matmul(fslots, ftok[...]).astype(jnp.bfloat16).reshape(experts, PAD, width)
    all_b[c, q, h] = placed_b[h]
    all_f[c, q, h] = placed_f[h]

    pl.semaphore_wait(barrier, len(others))

    def origin(k):
        return (h + experts - k) % experts

    def cross_send(s, placed, alls):
        for k in range(1, experts):
            send(
                placed.at[(h + k) % experts],
                alls.at[c, q, h],
                cross_s.at[s, k],
                cross_r.at[s, k],
                crosses[k],
            )

    def spread(s, alls, k, kind, part, dev):
        slot = alls.at[part[0], part[1], origin(k)]
        send(slot, slot, disp_s.at[s, k, kind], disp_r.at[s, k, kind], dev)

    def arrive(s, alls, k, kind, part, dev):
        slot = alls.at[part[0], part[1], origin(k)]
        rc(slot, slot, disp_s.at[s, k, kind], disp_r.at[s, k, kind], dev).wait_recv()

    def direct(s, alls, k):
        if k > 0:
            slot = alls.at[c, q, origin(k)]
            rc(slot, slot, cross_s.at[s, k], cross_r.at[s, k], crosses[k]).wait_recv()
        spread(s, alls, k, 0, (c, q), xn)
        spread(s, alls, k, 1, (c, q), zn)
        spread(s, alls, k, 2, (c, q), sib)

    def forward(s, alls, k):
        arrive(s, alls, k, 0, (c, qx), xn)
        if k % 2 == 0:
            spread(s, alls, k, 5, (c, qx), zn)
        spread(s, alls, k, 3, (c, qx), sib)
        arrive(s, alls, k, 1, (c, qz), zn)
        if k % 2 == 1:
            spread(s, alls, k, 5, (c, qz), xn)
        spread(s, alls, k, 4, (c, qz), sib)

    def last(s, alls, k):
        arrive(s, alls, k, 5, (c, qd), zn if k % 2 == 0 else xn)
        spread(s, alls, k, 6, (c, qd), sib)

    def complete(s, alls, k):
        arrive(s, alls, k, 2, (o, q), sib)
        arrive(s, alls, k, 3, (o, qx), sib)
        arrive(s, alls, k, 4, (o, qz), sib)
        arrive(s, alls, k, 6, (o, qd), sib)

    def mirror_send(k, at, quarter):
        j = origin(k)
        send(
            all_b.at[c, quarter, j, :, :, other_half],
            mirrored.at[c, quarter, j],
            pipe_s.at[k, at],
            pipe_r.at[k, at],
            mirror,
        )

    def mirror_arrive(k, at, quarter):
        j = origin(k)
        rc(
            all_b.at[c, quarter, j, :, :, other_half],
            mirrored.at[c, quarter, j],
            pipe_s.at[k, at],
            pipe_r.at[k, at],
            mirror,
        ).wait_recv()
        slot = mirrored.at[c, quarter, j]
        send(slot, slot, side_s.at[k, at], side_r.at[k, at], sib)

    def mirror_complete(k, at, quarter):
        slot = mirrored.at[o, quarter, origin(k)]
        rc(slot, slot, side_s.at[k, at], side_r.at[k, at], sib).wait_recv()

    quarters = (q, qx, qz, qd)

    cross_send(0, placed_b, all_b)
    direct(0, all_b, 0)
    mirror_send(0, 0, q)
    cross_send(1, placed_f, all_f)
    direct(1, all_f, 0)
    wgu[:, :hidden] = wg[...]
    wgu[:, hidden:] = wu[...]
    forward(0, all_b, 0)
    mirror_send(0, 1, qx)
    mirror_send(0, 2, qz)
    last(0, all_b, 0)
    mirror_send(0, 3, qd)
    for k in range(1, experts):
        direct(0, all_b, k)
        mirror_send(k, 0, q)
    forward(1, all_f, 0)
    last(1, all_f, 0)
    for k in range(1, experts):
        forward(0, all_b, k)
        mirror_send(k, 1, qx)
        mirror_send(k, 2, qz)
        direct(1, all_f, k)
    for k in range(1, experts):
        last(0, all_b, k)
        mirror_send(k, 3, qd)
    for at in range(4):
        mirror_arrive(0, at, quarters[at])
    for k in range(experts):
        complete(0, all_b, k)

    def columns(i, size):
        return pl.ds(pl.multiple_of(i * size, size), size)

    pre[...] = jnp.zeros_like(pre)
    hgrad[...] = jnp.zeros_like(hgrad)

    def backward_step(i, carry):
        at = columns(i, chunk)
        y = all_b[:, :, :, 0, :, at].reshape(rows, chunk)
        g = all_b[:, :, :, 1, :, at].reshape(rows, chunk)
        pre[...] += matmul(y, wgu[at, :])
        hgrad[...] += contract_last(g, wd[:, at])
        return carry

    lax.fori_loop(0, width // chunk, backward_step, 0)
    gate_pre = pre[:, :hidden]
    up_pre = pre[:, hidden:]
    sigma = 1.0 / (1.0 + jnp.exp(-gate_pre))
    activated = gate_pre * sigma
    hidden_grad = hgrad[...]
    grads[:, 2 * hidden :] = (activated * up_pre).astype(jnp.bfloat16)
    grads[:, :hidden] = (
        hidden_grad * up_pre * sigma * (1.0 + gate_pre * (1.0 - sigma))
    ).astype(jnp.bfloat16)
    grads[:, hidden : 2 * hidden] = (hidden_grad * activated).astype(jnp.bfloat16)
    send(grads, mgrads, pipe_s.at[0, 4], pipe_r.at[0, 4], mirror)

    for k in range(1, experts):
        forward(1, all_f, k)

    def weight_grads(first, count):
        def step(i, carry):
            to = columns(i, half_chunk)
            at = pl.ds(pl.multiple_of(side * middle + i * half_chunk, half_chunk), half_chunk)
            y = all_b[:, :, :, 0, :, at].reshape(rows, half_chunk)
            my = mirrored[:, :, :, 0, :, to].reshape(rows, half_chunk)
            both = matmul(y.T, grads[:, : 2 * hidden]) + matmul(my.T, mgrads[:, : 2 * hidden])
            out_g[to, :] = both[:, :hidden].astype(jnp.bfloat16)
            out_u[to, :] = both[:, hidden:].astype(jnp.bfloat16)
            g = all_b[:, :, :, 1, :, at].reshape(rows, half_chunk)
            mg = mirrored[:, :, :, 1, :, to].reshape(rows, half_chunk)
            out_d[:, to] = (
                matmul(grads[:, 2 * hidden :].T, g) + matmul(mgrads[:, 2 * hidden :].T, mg)
            ).astype(jnp.bfloat16)
            return carry

        lax.fori_loop(first, first + count, step, 0)

    for k in range(1, experts):
        last(1, all_f, k)

    def back_step(i, carry):
        at = columns(i, chunk)
        value = contract_last(grads[:, : 2 * hidden], wgu[at, :]).astype(jnp.bfloat16)
        parts[0, :, :, :, :, at] = value.reshape(2, 4, experts, PAD, chunk)
        return carry

    lax.fori_loop(0, width // chunk, back_step, 0)

    def to_sibling(s):
        send(parts.at[s, o], r1.at[s], ret_s.at[s, 0], ret_r.at[s, 0], sib)

    def pair_sum(s):
        rc(parts.at[s, o], r1.at[s], ret_s.at[s, 0], ret_r.at[s, 0], sib).wait_recv()

        def add(first):
            parts[s, c, first] = (
                parts[s, c, first].astype(jnp.float32) + r1[s, first].astype(jnp.float32)
            ).astype(jnp.bfloat16)

        add(qd)
        for j in range(experts):
            send(
                parts.at[s, c, qd, j],
                r2a.at[s, j],
                back_s.at[s, j, 0],
                back_r.at[s, j, 0],
                xn if j % 2 == 0 else zn,
            )
        add(qx)
        for j in range(0, experts, 2):
            send(
                parts.at[s, c, qx, j], r2x.at[s, j], back_s.at[s, j, 1], back_r.at[s, j, 1], xn
            )
        add(qz)
        for j in range(1, experts, 2):
            send(
                parts.at[s, c, qz, j], r2z.at[s, j], back_s.at[s, j, 2], back_r.at[s, j, 2], zn
            )
        add(q)

    def passed_on(s):
        for j in range(experts):
            even = j % 2 == 0
            rc(
                parts.at[s, c, qd, j],
                r2a.at[s, j],
                back_s.at[s, j, 0],
                back_r.at[s, j, 0],
                xn if even else zn,
            ).wait_recv()
            to = qz if even else qx
            parts[s, c, to, j] = (
                parts[s, c, to, j].astype(jnp.float32) + r2a[s, j].astype(jnp.float32)
            ).astype(jnp.bfloat16)
            if even:
                send(
                    parts.at[s, c, qz, j], r2z.at[s, j], back_s.at[s, j, 2], back_r.at[s, j, 2], zn
                )
            else:
                send(
                    parts.at[s, c, qx, j], r2x.at[s, j], back_s.at[s, j, 1], back_r.at[s, j, 1], xn
                )

    def summed(s):
        for j in range(experts):
            rc(
                parts.at[s, c, qx, j], r2x.at[s, j], back_s.at[s, j, 1], back_r.at[s, j, 1], xn
            ).wait_recv()
            rc(
                parts.at[s, c, qz, j], r2z.at[s, j], back_s.at[s, j, 2], back_r.at[s, j, 2], zn
            ).wait_recv()
            tsend[s, j] = (
                parts[s, c, q, j].astype(jnp.float32)
                + r2x[s, j].astype(jnp.float32)
                + r2z[s, j].astype(jnp.float32)
            ).astype(jnp.bfloat16)
        for k in range(1, experts):
            send(
                tsend.at[s, (h + k) % experts],
                r3.at[s, h],
                ret_s.at[s, k],
                ret_r.at[s, k],
                crosses[k],
            )
        r3[s, h] = tsend[s, h]

    def home(s):
        for k in range(1, experts):
            slot = r3.at[s, origin(k)]
            rc(slot, slot, ret_s.at[s, k], ret_r.at[s, k], crosses[k]).wait_recv()
        return r3[s].reshape(experts * PAD, width)

    to_sibling(0)
    for k in range(1, experts):
        for at in range(4):
            mirror_arrive(k, at, quarters[at])

    for k in range(experts):
        complete(1, all_f, k)
    pre[...] = jnp.zeros_like(pre)

    def forward_step(i, carry):
        at = columns(i, chunk)
        x = all_f[:, :, :, 0, :, at].reshape(rows, chunk)
        pre[...] += matmul(x, wgu[at, :])
        return carry

    lax.fori_loop(0, width // chunk, forward_step, 0)
    fgate_pre = pre[:, :hidden]
    fhid = ((fgate_pre / (1.0 + jnp.exp(-fgate_pre))) * pre[:, hidden:]).astype(jnp.bfloat16)
    pair_sum(0)

    hgrad[...] = fhid.astype(jnp.float32)

    def parts_step(i, carry):
        at = columns(i, chunk)
        value = matmul(hgrad[...].astype(jnp.bfloat16), wd[:, at]).astype(jnp.bfloat16)
        parts[1, :, :, :, :, at] = value.reshape(2, 4, experts, PAD, chunk)
        return carry

    lax.fori_loop(0, width // chunk, parts_step, 0)
    to_sibling(1)
    passed_on(0)
    pair_sum(1)
    summed(0)
    passed_on(1)
    rc(grads, mgrads, pipe_s.at[0, 4], pipe_r.at[0, 4], mirror).wait_recv()
    for k in range(experts):
        for at in range(4):
            mirror_complete(k, at, quarters[at])
    weight_grads(0, middle // half_chunk)
    summed(1)

    at_place_t = lax.broadcasted_iota(jnp.int32, (ftok.shape[0], experts * PAD), 1)
    bslots_t = jnp.where(at_place_t == bplace_col, 1.0, 0.0).astype(jnp.bfloat16)
    fslots_t = jnp.where(at_place_t == fplace_col, 1.0, 0.0).astype(jnp.bfloat16)
    out_b[...] = matmul(bslots_t, home(0)).astype(jnp.bfloat16)
    gated = (fgate_place * home(1).astype(jnp.float32)).astype(jnp.bfloat16)
    out_f[...] = matmul(fslots_t, gated).astype(jnp.bfloat16)

    for copy in sent:
        copy.wait_send()


def hand_out(*refs):
    copies = [pltpu.make_async_copy(refs[i], refs[5 + i], refs[10].at[i]) for i in range(5)]
    for copy in copies:
        copy.start()
    for copy in copies:
        copy.wait()


def on_device(
    forward_tokens,
    forward_routing,
    forward_gates,
    backward_tokens,
    backward_routing,
    backward_gates,
    cotangent,
    gate_matrix,
    up_matrix,
    down_matrix,
):
    devices = lax.axis_size("expert")
    positions = lax.axis_size("pipe")
    experts = devices // SHARING_CARDS
    tokens, width = forward_tokens.shape[1:]
    hidden = gate_matrix.shape[2]
    middle = width // 2
    rows = SHARING_CARDS * experts * PAD
    bf16, f32 = jnp.bfloat16, jnp.float32
    vmem = pl.BlockSpec(memory_space=pltpu.VMEM)
    dma = pltpu.SemaphoreType.DMA
    outs = pl.pallas_call(
        functools.partial(kernel, experts, positions),
        out_shape=(
            jax.ShapeDtypeStruct((tokens, width), bf16),
            jax.ShapeDtypeStruct((tokens, width), bf16),
            jax.ShapeDtypeStruct((middle, hidden), bf16),
            jax.ShapeDtypeStruct((middle, hidden), bf16),
            jax.ShapeDtypeStruct((hidden, middle), bf16),
        ),
        in_specs=[vmem] * 10,
        out_specs=(vmem,) * 5,
        scratch_shapes=[
            pltpu.VMEM((width, 2 * hidden), bf16),
            pltpu.VMEM((experts, 2, PAD, width), bf16),
            pltpu.VMEM((experts, 1, PAD, width), bf16),
            pltpu.VMEM((2, 4, experts, 2, PAD, width), bf16),
            pltpu.VMEM((2, 4, experts, 1, PAD, width), bf16),
            pltpu.VMEM((2, 2, 4, experts, PAD, width), bf16),
            pltpu.VMEM((2, 4, experts, PAD, width), bf16),
            pltpu.VMEM((2, experts, PAD, width), bf16),
            pltpu.VMEM((2, experts, PAD, width), bf16),
            pltpu.VMEM((2, experts, PAD, width), bf16),
            pltpu.VMEM((2, experts, PAD, width), bf16),
            pltpu.VMEM((2, experts, PAD, width), bf16),
            pltpu.VMEM((rows, 2 * hidden), f32),
            pltpu.VMEM((rows, hidden), f32),
            pltpu.VMEM((rows, 3 * hidden), bf16),
            pltpu.VMEM((rows, 3 * hidden), bf16),
            pltpu.VMEM((2, 4, experts, 2, PAD, middle), bf16),
            dma((2, experts)),
            dma((2, experts)),
            dma((2, experts, 7)),
            dma((2, experts, 7)),
            dma((2, experts)),
            dma((2, experts)),
            dma((2, experts, 3)),
            dma((2, experts, 3)),
            dma((experts, 5)),
            dma((experts, 5)),
            dma((experts, 4)),
            dma((experts, 4)),
        ],
        compiler_params=pltpu.CompilerParams(
            collective_id=0, has_side_effects=True, vmem_limit_bytes=40 * 1024 * 1024
        ),
    )(
        forward_tokens[0],
        forward_routing.reshape(1, tokens),
        forward_gates,
        backward_tokens[0],
        backward_routing.reshape(1, tokens),
        backward_gates,
        cotangent[0],
        gate_matrix[0],
        up_matrix[0],
        down_matrix[0],
    )
    outs = pl.pallas_call(
        hand_out,
        out_shape=tuple(jax.ShapeDtypeStruct(out.shape, bf16) for out in outs),
        in_specs=[pl.BlockSpec(memory_space=pl.ANY)] * 5,
        out_specs=(pl.BlockSpec(memory_space=pl.ANY),) * 5,
        scratch_shapes=[dma((5,))],
        compiler_params=pltpu.CompilerParams(vmem_limit_bytes=1024 * 1024),
    )(*outs)
    return tuple(out[None] for out in outs)


def solution(mesh):
    in_specs = (
        P("pipe", "expert", None),
        P("pipe", "expert", None),
        P("pipe", "expert"),
        P("pipe", "expert", None),
        P("pipe", "expert", None),
        P("pipe", "expert"),
        P("pipe", "expert", None),
        P("pipe", None, "expert"),
        P("pipe", None, "expert"),
        P("pipe", "expert", None),
    )
    out_specs = (
        P("pipe", "expert", None),
        P("pipe", "expert", None),
        P("pipe", None, "expert"),
        P("pipe", None, "expert"),
        P("pipe", "expert", None),
    )
    return jax.shard_map(
        on_device, mesh=mesh, in_specs=in_specs, out_specs=out_specs, check_vma=False
    )
```

```python
import functools

import jax
import jax.numpy as jnp
from jax import lax
from jax.experimental import pallas as pl
from jax.experimental.pallas import tpu as pltpu
from jax.sharding import PartitionSpec as P

SHARING_CARDS = 8
PAD = 16
SLOTS = 12
BLOCK = 32
MESH = pl.DeviceIdType.MESH


def flip(value, bit):
    return value + bit - 2 * bit * ((value // bit) % 2)


def contract_last(left, right):
    return lax.dot_general(
        left, right, (((1,), (1,)), ((), ())), preferred_element_type=jnp.float32
    )


def matmul(left, right):
    return jnp.dot(left, right, preferred_element_type=jnp.float32)


def row_and_column(row):
    n = row.shape[1]
    at0 = lax.broadcasted_iota(jnp.int32, (n, n), 0)
    at1 = lax.broadcasted_iota(jnp.int32, (n, n), 1)
    return jnp.sum(jnp.where(at0 == at1, row, jnp.zeros_like(row)), axis=1, keepdims=True)


def within(routing_row):
    n = routing_row.shape[1]
    column = row_and_column(routing_row)
    at0 = lax.broadcasted_iota(jnp.int32, (n, n), 0)
    at1 = lax.broadcasted_iota(jnp.int32, (n, n), 1)
    same = column == routing_row
    before_row = jnp.sum(jnp.where(same & (at0 < at1), 1.0, 0.0), axis=0, keepdims=True)
    before_column = jnp.sum(jnp.where(same & (at1 < at0), 1.0, 0.0), axis=1, keepdims=True)
    return before_row.astype(jnp.int32), column, before_column.astype(jnp.int32)


def one_hot(condition):
    return jnp.where(condition, 1.0, 0.0).astype(jnp.bfloat16)


def kernel(
    experts,
    positions,
    ftok,
    froute,
    fgate,
    btok,
    broute,
    bgate,
    cot,
    wg,
    wu,
    wd_far,
    out_f,
    out_b,
    out_g,
    out_u,
    out_d,
    wgu,
    wd,
    placed_b,
    placed_f,
    all_b,
    all_f,
    parts,
    r1,
    r2a,
    r2x,
    r2z,
    tsend,
    r3,
    pre,
    hgrad,
    grads,
    mgrads,
    spaced,
    grads_t,
    mgrads_t,
    left1,
    left2,
    mirrored,
    weight_s,
    cross_s,
    cross_r,
    disp_s,
    disp_r,
    ret_s,
    ret_r,
    back_s,
    back_r,
    pipe_s,
    pipe_r,
    side_s,
    side_r,
):
    tokens, width = ftok.shape
    hidden = wg.shape[1]
    middle = width // 2
    quarter = width // 4
    chunk = 256
    steps = middle // chunk
    blocks = SHARING_CARDS * experts
    rows = blocks * PAD
    long_rows = blocks * BLOCK
    e = lax.axis_index("expert")
    p = lax.axis_index("pipe")
    h = e // SHARING_CARDS
    m = e % SHARING_CARDS
    base = h * SHARING_CARDS
    c = m % 2
    o = 1 - c
    q = m // 2
    qx, qz = flip(q, 1), flip(q, 2)
    qd = flip(qx, 2)
    sib = {"expert": base + flip(m, 1)}
    xn = {"expert": base + flip(m, 2)}
    zn = {"expert": base + flip(m, 4)}
    mirror = {"pipe": positions - 1 - p}
    side = p // (positions // 2)
    crosses = [{"expert": ((h + k) % experts) * SHARING_CARDS + m} for k in range(experts)]

    barrier = pltpu.get_barrier_semaphore()
    others = [sib, xn, zn, mirror] + crosses[1:]
    for other in others:
        pl.semaphore_signal(barrier, inc=1, device_id=other, device_id_type=MESH)

    weight_copies = [
        pltpu.make_async_copy(wg, wgu.at[:, pl.ds(0, hidden)], weight_s.at[0]),
        pltpu.make_async_copy(wu, wgu.at[:, pl.ds(hidden, hidden)], weight_s.at[1]),
        pltpu.make_async_copy(wd_far, wd, weight_s.at[2]),
    ]
    for copy in weight_copies:
        copy.start()

    def rc(src, dst, ss, rs, dev):
        return pltpu.make_async_remote_copy(
            src_ref=src, dst_ref=dst, send_sem=ss, recv_sem=rs, device_id=dev, device_id_type=MESH
        )

    sent = []

    def send(src, dst, ss, rs, dev):
        copy = rc(src, dst, ss, rs, dev)
        copy.start()
        sent.append(copy)

    broute_row, froute_row = broute[...], froute[...]
    bw_row, broute_col, bw_col = within(broute_row)
    fw_row, froute_col, fw_col = within(froute_row)
    at_long = lax.broadcasted_iota(jnp.int32, (experts * BLOCK, tokens), 0)
    at_short = lax.broadcasted_iota(jnp.int32, (experts * PAD, tokens), 0)
    y_slots = one_hot(at_long == broute_row * BLOCK + bw_row)
    g_slots = one_hot(at_long == broute_row * BLOCK + SLOTS + bw_row)
    x_slots = one_hot((at_long == froute_row * BLOCK + 2 * SLOTS + fw_row) & (fw_row < 8))
    scaled = (row_and_column(bgate[...]) * cot[...].astype(jnp.float32)).astype(jnp.bfloat16)
    for half in range(2):
        at = pl.ds(half * middle, middle)
        placed_b[half] = (
            (
                matmul(y_slots, btok[:, at])
                + matmul(g_slots, scaled[:, half * middle : (half + 1) * middle])
                + matmul(x_slots, ftok[:, at])
            )
            .astype(jnp.bfloat16)
            .reshape(experts, BLOCK, middle)
        )
        all_b[half, c, q, h] = placed_b[half, h]
    tail = jnp.zeros((experts * PAD, quarter), jnp.float32)
    for part in range(4):
        slots = one_hot((at_short == froute_row * PAD + 4 * part + fw_row - 8) & (fw_row >= 8))
        tail = tail + matmul(slots, ftok[:, pl.ds(part * quarter, quarter)])
    placed_f[...] = tail.astype(jnp.bfloat16).reshape(experts, PAD, quarter)
    all_f[c, q, h] = placed_f[h]

    pl.semaphore_wait(barrier, len(others))

    streams = (
        (placed_b.at[0], all_b.at[0]),
        (placed_b.at[1], all_b.at[1]),
        (placed_f, all_f),
    )

    def origin(k):
        return (h + experts - k) % experts

    def cross_send(s):
        placed, alls = streams[s]
        for k in range(1, experts):
            send(
                placed.at[(h + k) % experts],
                alls.at[c, q, h],
                cross_s.at[s, k],
                cross_r.at[s, k],
                crosses[k],
            )

    def spread(s, k, kind, part, dev):
        slot = streams[s][1].at[part[0], part[1], origin(k)]
        send(slot, slot, disp_s.at[s, k, kind], disp_r.at[s, k, kind], dev)

    def arrive(s, k, kind, part, dev):
        slot = streams[s][1].at[part[0], part[1], origin(k)]
        rc(slot, slot, disp_s.at[s, k, kind], disp_r.at[s, k, kind], dev).wait_recv()

    def direct(s, k):
        if k > 0:
            slot = streams[s][1].at[c, q, origin(k)]
            rc(slot, slot, cross_s.at[s, k], cross_r.at[s, k], crosses[k]).wait_recv()
        spread(s, k, 0, (c, q), xn)
        spread(s, k, 1, (c, q), zn)
        spread(s, k, 2, (c, q), sib)

    def forward(s, k):
        arrive(s, k, 0, (c, qx), xn)
        if k % 2 == 0:
            spread(s, k, 5, (c, qx), zn)
        spread(s, k, 3, (c, qx), sib)
        arrive(s, k, 1, (c, qz), zn)
        if k % 2 == 1:
            spread(s, k, 5, (c, qz), xn)
        spread(s, k, 4, (c, qz), sib)

    def last(s, k):
        arrive(s, k, 5, (c, qd), zn if k % 2 == 0 else xn)
        spread(s, k, 6, (c, qd), sib)

    def complete(s, k):
        arrive(s, k, 2, (o, q), sib)
        arrive(s, k, 3, (o, qx), sib)
        arrive(s, k, 4, (o, qz), sib)
        arrive(s, k, 6, (o, qd), sib)

    quarters = (q, qx, qz, qd)

    def mirror_copy(k, at):
        j, own = origin(k), quarters[at]
        return (
            all_b.at[1 - side, c, own, j],
            mirrored.at[c, own, j],
            pipe_s.at[k, at],
            pipe_r.at[k, at],
            mirror,
        )

    def mirror_send(k, at):
        send(*mirror_copy(k, at))

    def mirror_arrive(k, at):
        rc(*mirror_copy(k, at)).wait_recv()
        slot = mirrored.at[c, quarters[at], origin(k)]
        send(slot, slot, side_s.at[k, at], side_r.at[k, at], sib)

    def mirror_complete(k, at):
        slot = mirrored.at[o, quarters[at], origin(k)]
        rc(slot, slot, side_s.at[k, at], side_r.at[k, at], sib).wait_recv()

    later = range(1, experts)
    for s in range(3):
        cross_send(s)
        direct(s, 0)
    mirror_send(0, 0)
    forward(0, 0)
    forward(1, 0)
    mirror_send(0, 1)
    mirror_send(0, 2)
    for k in later:
        direct(0, k)
    last(0, 0)
    last(1, 0)
    mirror_send(0, 3)
    forward(2, 0)
    for k in later:
        direct(1, k)
        mirror_send(k, 0)
        direct(2, k)
    last(2, 0)
    for k in later:
        forward(0, k)
    for k in later:
        forward(1, k)
        mirror_send(k, 1)
        mirror_send(k, 2)
        forward(2, k)
    for k in later:
        for s in range(3):
            last(s, k)
        mirror_send(k, 3)
    for copy in weight_copies:
        copy.wait()
    for k in range(experts):
        for s in range(3):
            complete(s, k)

    def columns(i):
        return pl.ds(pl.multiple_of(i * chunk, chunk), chunk)

    def far_columns(start, i):
        return pl.ds(pl.multiple_of(start + i * chunk, chunk), chunk)

    pre[...] = jnp.zeros_like(pre)
    hgrad[...] = jnp.zeros_like(hgrad)

    def first_step(i, carry):
        for half in range(2):
            at = far_columns(half * middle, i)
            block = all_b[half, :, :, :, :, columns(i)].reshape(long_rows, chunk)
            pre[...] += matmul(block, wgu[at, :])
            hgrad[...] += contract_last(block, wd[:, at])
        return carry

    lax.fori_loop(0, steps, first_step, 0)

    def part_of(value, start):
        return value.reshape(blocks, BLOCK, value.shape[1])[:, start : start + PAD].reshape(
            rows, value.shape[1]
        )

    in_block = lax.broadcasted_iota(jnp.int32, (rows, 1), 0) % PAD
    valid = in_block < SLOTS
    pre_y = part_of(pre[...], 0)
    gate_pre, up_pre = pre_y[:, :hidden], pre_y[:, hidden:]
    hidden_grad = part_of(pltpu.roll(hgrad[...], long_rows - SLOTS, 0), 0)
    sigma = 1.0 / (1.0 + jnp.exp(-gate_pre))
    activated = gate_pre * sigma
    grads[:, 2 * hidden :] = jnp.where(valid, activated * up_pre, 0.0).astype(jnp.bfloat16)
    grads[:, :hidden] = jnp.where(
        valid, hidden_grad * up_pre * sigma * (1.0 + gate_pre * (1.0 - sigma)), 0.0
    ).astype(jnp.bfloat16)
    grads[:, hidden : 2 * hidden] = jnp.where(valid, hidden_grad * activated, 0.0).astype(
        jnp.bfloat16
    )
    send(grads, mgrads, pipe_s.at[0, 4], pipe_r.at[0, 4], mirror)

    def silu_product(value):
        gate, up = value[:, :hidden], value[:, hidden:]
        return gate / (1.0 + jnp.exp(-gate)) * up

    short = all_f[...].reshape(rows, quarter)
    pre_f = matmul(short, wgu[pl.ds(0, quarter), :])
    for part in range(1, 4):
        partial = matmul(short, wgu[pl.ds(part * quarter, quarter), :])
        pre_f = pre_f + pltpu.roll(partial, rows - 4 * part, 0)
    left1[...] = jnp.where(valid, 0.0, pltpu.roll(silu_product(pre_f), SLOTS, 0)).astype(
        jnp.bfloat16
    )
    hid8 = silu_product(part_of(pre[...], PAD))
    left2[:, :hidden] = jnp.where(in_block < 8, pltpu.roll(hid8, rows - 8, 0), 0.0).astype(
        jnp.bfloat16
    )
    left2[:, hidden:] = jnp.where(in_block < 8, 0.0, hid8).astype(jnp.bfloat16)

    def make_parts(s):
        def step(i, carry):
            at = columns(i)
            if s < 2:
                far = far_columns(s * middle, i)
                value = contract_last(grads[:, : 2 * hidden], wgu[far, :])
                value = value + matmul(left1[...], wd[:, far])
            else:
                value = matmul(left2[:, :hidden], wd[:, at])
                value = value + matmul(left2[:, hidden:], wd[:, far_columns(middle, i)])
            parts[s, :, :, :, :, at] = value.astype(jnp.bfloat16).reshape(
                2, 4, experts, PAD, chunk
            )
            return carry

        lax.fori_loop(0, steps, step, 0)
        send(parts.at[s, o], r1.at[s], ret_s.at[s, 0], ret_r.at[s, 0], sib)

    def pass_copy(s, j):
        return (
            parts.at[s, c, qd, j],
            r2a.at[s, j],
            back_s.at[s, j, 0],
            back_r.at[s, j, 0],
            xn if j % 2 == 0 else zn,
        )

    def x_copy(s, j):
        return parts.at[s, c, qx, j], r2x.at[s, j], back_s.at[s, j, 1], back_r.at[s, j, 1], xn

    def z_copy(s, j):
        return parts.at[s, c, qz, j], r2z.at[s, j], back_s.at[s, j, 2], back_r.at[s, j, 2], zn

    def pair_sum(s):
        rc(parts.at[s, o], r1.at[s], ret_s.at[s, 0], ret_r.at[s, 0], sib).wait_recv()

        def add(first):
            parts[s, c, first] = (
                parts[s, c, first].astype(jnp.float32) + r1[s, first].astype(jnp.float32)
            ).astype(jnp.bfloat16)

        add(qd)
        for j in range(experts):
            send(*pass_copy(s, j))
        add(qx)
        for j in range(0, experts, 2):
            send(*x_copy(s, j))
        add(qz)
        for j in range(1, experts, 2):
            send(*z_copy(s, j))
        add(q)

    def passed_on(s):
        for j in range(experts):
            even = j % 2 == 0
            rc(*pass_copy(s, j)).wait_recv()
            to = qz if even else qx
            parts[s, c, to, j] = (
                parts[s, c, to, j].astype(jnp.float32) + r2a[s, j].astype(jnp.float32)
            ).astype(jnp.bfloat16)
            if even:
                send(*z_copy(s, j))
            else:
                send(*x_copy(s, j))

    def summed(s):
        for j in range(experts):
            rc(*x_copy(s, j)).wait_recv()
            rc(*z_copy(s, j)).wait_recv()
            tsend[s, j] = (
                parts[s, c, q, j].astype(jnp.float32)
                + r2x[s, j].astype(jnp.float32)
                + r2z[s, j].astype(jnp.float32)
            ).astype(jnp.bfloat16)
        for k in later:
            send(
                tsend.at[s, (h + k) % experts],
                r3.at[s, h],
                ret_s.at[s, k],
                ret_r.at[s, k],
                crosses[k],
            )
        r3[s, h] = tsend[s, h]

    def home(s):
        for k in later:
            slot = r3.at[s, origin(k)]
            rc(slot, slot, ret_s.at[s, k], ret_r.at[s, k], crosses[k]).wait_recv()
        return r3[s].reshape(experts * PAD, middle)

    def transposed(source, target):
        spaced[:, :PAD] = source[...].reshape(blocks, PAD, 3 * hidden)
        spaced[:, PAD:] = jnp.zeros((blocks, BLOCK - PAD, 3 * hidden), jnp.bfloat16)
        full = spaced[...].reshape(long_rows, 3 * hidden)
        target[: 2 * hidden, :] = full[:, : 2 * hidden].T
        down = pltpu.roll(full[:, 2 * hidden :].astype(jnp.float32), SLOTS, 0)
        target[2 * hidden :, :] = down.astype(jnp.bfloat16).T

    def weight_grads(first, end):
        def step(i, carry):
            at = columns(i)
            block = all_b[side, :, :, :, :, at].reshape(long_rows, chunk)
            far = mirrored[:, :, :, :, at].reshape(long_rows, chunk)
            total = matmul(grads_t[...], block) + matmul(mgrads_t[...], far)
            both = total[: 2 * hidden].T.astype(jnp.bfloat16)
            out_g[at, :] = both[:, :hidden]
            out_u[at, :] = both[:, hidden:]
            out_d[:, at] = total[2 * hidden :].astype(jnp.bfloat16)
            return carry

        lax.fori_loop(first, end, step, 0)

    make_parts(0)
    make_parts(1)
    pair_sum(0)
    make_parts(2)
    pair_sum(1)
    for k in range(experts):
        for at in range(4):
            mirror_arrive(k, at)
    passed_on(0)
    pair_sum(2)
    transposed(grads, grads_t)
    passed_on(1)
    rc(grads, mgrads, pipe_s.at[0, 4], pipe_r.at[0, 4], mirror).wait_recv()
    transposed(mgrads, mgrads_t)
    for k in range(experts):
        for at in range(4):
            mirror_complete(k, at)
    summed(0)
    passed_on(2)
    weight_grads(0, steps // 2)
    summed(1)
    weight_grads(steps // 2, steps)
    summed(2)

    at_t = lax.broadcasted_iota(jnp.int32, (tokens, experts * PAD), 1)
    b_slots = one_hot(at_t == broute_col * PAD + bw_col)
    f_last = one_hot((at_t == froute_col * PAD + fw_col + 4) & (fw_col >= 8))
    f_left = one_hot((at_t == froute_col * PAD + fw_col) & (fw_col < 8))
    f_right = one_hot((at_t == froute_col * PAD + fw_col + 8) & (fw_col < 8))
    fgate_col = row_and_column(fgate[...])
    first = home(0)
    out_b[:, :middle] = matmul(b_slots, first).astype(jnp.bfloat16)
    second = home(1)
    out_b[:, middle:] = matmul(b_slots, second).astype(jnp.bfloat16)
    third = home(2)
    out_f[:, :middle] = (fgate_col * (matmul(f_last, first) + matmul(f_left, third))).astype(
        jnp.bfloat16
    )
    out_f[:, middle:] = (fgate_col * (matmul(f_last, second) + matmul(f_right, third))).astype(
        jnp.bfloat16
    )
    for copy in sent:
        copy.wait_send()


def hand_out(*refs):
    copies = [pltpu.make_async_copy(refs[i], refs[5 + i], refs[10].at[i]) for i in range(5)]
    for copy in copies:
        copy.start()
    for copy in copies:
        copy.wait()


def on_device(
    forward_tokens,
    forward_routing,
    forward_gates,
    backward_tokens,
    backward_routing,
    backward_gates,
    cotangent,
    gate_matrix,
    up_matrix,
    down_matrix,
):
    devices = lax.axis_size("expert")
    positions = lax.axis_size("pipe")
    experts = devices // SHARING_CARDS
    tokens, width = forward_tokens.shape[1:]
    hidden = gate_matrix.shape[2]
    middle = width // 2
    blocks = SHARING_CARDS * experts
    rows = blocks * PAD
    assert max(tokens // 3, tokens // experts) <= SLOTS
    bf16, f32 = jnp.bfloat16, jnp.float32
    vmem = pl.BlockSpec(memory_space=pltpu.VMEM)
    far = pl.BlockSpec(memory_space=pl.ANY)
    dma = pltpu.SemaphoreType.DMA
    outs = pl.pallas_call(
        functools.partial(kernel, experts, positions),
        out_shape=(
            jax.ShapeDtypeStruct((tokens, width), bf16),
            jax.ShapeDtypeStruct((tokens, width), bf16),
            jax.ShapeDtypeStruct((middle, hidden), bf16),
            jax.ShapeDtypeStruct((middle, hidden), bf16),
            jax.ShapeDtypeStruct((hidden, middle), bf16),
        ),
        in_specs=[vmem] * 7 + [far] * 3,
        out_specs=(vmem,) * 5,
        scratch_shapes=[
            pltpu.VMEM((width, 2 * hidden), bf16),
            pltpu.VMEM((hidden, width), bf16),
            pltpu.VMEM((2, experts, BLOCK, middle), bf16),
            pltpu.VMEM((experts, PAD, width // 4), bf16),
            pltpu.VMEM((2, 2, 4, experts, BLOCK, middle), bf16),
            pltpu.VMEM((2, 4, experts, PAD, width // 4), bf16),
            pltpu.VMEM((3, 2, 4, experts, PAD, middle), bf16),
            pltpu.VMEM((3, 4, experts, PAD, middle), bf16),
            pltpu.VMEM((3, experts, PAD, middle), bf16),
            pltpu.VMEM((3, experts, PAD, middle), bf16),
            pltpu.VMEM((3, experts, PAD, middle), bf16),
            pltpu.VMEM((3, experts, PAD, middle), bf16),
            pltpu.VMEM((3, experts, PAD, middle), bf16),
            pltpu.VMEM((blocks * BLOCK, 2 * hidden), f32),
            pltpu.VMEM((blocks * BLOCK, hidden), f32),
            pltpu.VMEM((rows, 3 * hidden), bf16),
            pltpu.VMEM((rows, 3 * hidden), bf16),
            pltpu.VMEM((blocks, BLOCK, 3 * hidden), bf16),
            pltpu.VMEM((3 * hidden, blocks * BLOCK), bf16),
            pltpu.VMEM((3 * hidden, blocks * BLOCK), bf16),
            pltpu.VMEM((rows, hidden), bf16),
            pltpu.VMEM((rows, 2 * hidden), bf16),
            pltpu.VMEM((2, 4, experts, BLOCK, middle), bf16),
            dma((3,)),
            dma((3, experts)),
            dma((3, experts)),
            dma((3, experts, 7)),
            dma((3, experts, 7)),
            dma((3, experts)),
            dma((3, experts)),
            dma((3, experts, 3)),
            dma((3, experts, 3)),
            dma((experts, 5)),
            dma((experts, 5)),
            dma((experts, 4)),
            dma((experts, 4)),
        ],
        compiler_params=pltpu.CompilerParams(
            collective_id=0, has_side_effects=True, vmem_limit_bytes=60 * 1024 * 1024
        ),
    )(
        forward_tokens[0],
        forward_routing.reshape(1, tokens),
        forward_gates,
        backward_tokens[0],
        backward_routing.reshape(1, tokens),
        backward_gates,
        cotangent[0],
        gate_matrix[0],
        up_matrix[0],
        down_matrix[0],
    )
    outs = pl.pallas_call(
        hand_out,
        out_shape=tuple(jax.ShapeDtypeStruct(out.shape, bf16) for out in outs),
        in_specs=[pl.BlockSpec(memory_space=pl.ANY)] * 5,
        out_specs=(pl.BlockSpec(memory_space=pl.ANY),) * 5,
        scratch_shapes=[dma((5,))],
        compiler_params=pltpu.CompilerParams(vmem_limit_bytes=60 * 1024 * 1024),
    )(*outs)
    return tuple(out[None] for out in outs)


def solution(mesh):
    in_specs = (
        P("pipe", "expert", None),
        P("pipe", "expert", None),
        P("pipe", "expert"),
        P("pipe", "expert", None),
        P("pipe", "expert", None),
        P("pipe", "expert"),
        P("pipe", "expert", None),
        P("pipe", None, "expert"),
        P("pipe", None, "expert"),
        P("pipe", "expert", None),
    )
    out_specs = (
        P("pipe", "expert", None),
        P("pipe", "expert", None),
        P("pipe", None, "expert"),
        P("pipe", None, "expert"),
        P("pipe", "expert", None),
    )
    return jax.shard_map(
        on_device, mesh=mesh, in_specs=in_specs, out_specs=out_specs, check_vma=False
    )
```

```python
import functools

import jax
import jax.numpy as jnp
from jax import lax
from jax.experimental import pallas as pl
from jax.experimental.pallas import tpu as pltpu
from jax.sharding import PartitionSpec as P

SHARING_CARDS = 8
PAD = 16
SLOTS = 12
BLOCK = 32
MESH = pl.DeviceIdType.MESH


def flip(value, bit):
    return value + bit - 2 * bit * ((value // bit) % 2)


def contract_last(left, right):
    return lax.dot_general(
        left, right, (((1,), (1,)), ((), ())), preferred_element_type=jnp.float32
    )


def matmul(left, right):
    return jnp.dot(left, right, preferred_element_type=jnp.float32)


def row_and_column(row):
    n = row.shape[1]
    at0 = lax.broadcasted_iota(jnp.int32, (n, n), 0)
    at1 = lax.broadcasted_iota(jnp.int32, (n, n), 1)
    return jnp.sum(jnp.where(at0 == at1, row, jnp.zeros_like(row)), axis=1, keepdims=True)


def within(routing_row):
    n = routing_row.shape[1]
    column = row_and_column(routing_row)
    at0 = lax.broadcasted_iota(jnp.int32, (n, n), 0)
    at1 = lax.broadcasted_iota(jnp.int32, (n, n), 1)
    same = column == routing_row
    before_row = jnp.sum(jnp.where(same & (at0 < at1), 1.0, 0.0), axis=0, keepdims=True)
    before_column = jnp.sum(jnp.where(same & (at1 < at0), 1.0, 0.0), axis=1, keepdims=True)
    return before_row.astype(jnp.int32), column, before_column.astype(jnp.int32)


def one_hot(condition):
    return jnp.where(condition, 1.0, 0.0).astype(jnp.bfloat16)


def kernel(
    experts,
    positions,
    ftok,
    froute,
    fgate,
    btok,
    broute,
    bgate,
    cot,
    wg,
    wu,
    wd_far,
    out_f,
    out_b,
    out_g,
    out_u,
    out_d,
    wgu,
    wd,
    placed_b,
    placed_f,
    all_b,
    all_f,
    parts,
    r1,
    r2a,
    r2x,
    r2z,
    tsend,
    r3,
    pre,
    hgrad,
    grads,
    mgrads,
    spaced,
    grads_t,
    mgrads_t,
    left1,
    left2,
    mirrored,
    weight_s,
    cross_s,
    cross_r,
    disp_s,
    disp_r,
    ret_s,
    ret_r,
    back_s,
    back_r,
    pipe_s,
    pipe_r,
    side_s,
    side_r,
):
    tokens, width = ftok.shape
    hidden = wg.shape[1]
    middle = width // 2
    quarter = width // 4
    chunk = 256
    steps = middle // chunk
    blocks = SHARING_CARDS * experts
    rows = blocks * PAD
    long_rows = blocks * BLOCK
    e = lax.axis_index("expert")
    p = lax.axis_index("pipe")
    h = e // SHARING_CARDS
    m = e % SHARING_CARDS
    base = h * SHARING_CARDS
    c = m % 2
    o = 1 - c
    q = m // 2
    qx, qz = flip(q, 1), flip(q, 2)
    qd = flip(qx, 2)
    sib = {"expert": base + flip(m, 1)}
    xn = {"expert": base + flip(m, 2)}
    zn = {"expert": base + flip(m, 4)}
    mirror = {"pipe": positions - 1 - p}
    side = p // (positions // 2)
    crosses = [{"expert": ((h + k) % experts) * SHARING_CARDS + m} for k in range(experts)]

    barrier = pltpu.get_barrier_semaphore()
    others = [sib, xn, zn, mirror] + crosses[1:]
    for other in others:
        pl.semaphore_signal(barrier, inc=1, device_id=other, device_id_type=MESH)

    weight_copies = [
        pltpu.make_async_copy(wg, wgu.at[:, pl.ds(0, hidden)], weight_s.at[0]),
        pltpu.make_async_copy(wu, wgu.at[:, pl.ds(hidden, hidden)], weight_s.at[1]),
        pltpu.make_async_copy(wd_far, wd, weight_s.at[2]),
    ]
    for copy in weight_copies:
        copy.start()

    def rc(src, dst, ss, rs, dev):
        return pltpu.make_async_remote_copy(
            src_ref=src, dst_ref=dst, send_sem=ss, recv_sem=rs, device_id=dev, device_id_type=MESH
        )

    sent = []

    def send(src, dst, ss, rs, dev):
        copy = rc(src, dst, ss, rs, dev)
        copy.start()
        sent.append(copy)

    broute_row, froute_row = broute[...], froute[...]
    bw_row, broute_col, bw_col = within(broute_row)
    fw_row, froute_col, fw_col = within(froute_row)
    at_long = lax.broadcasted_iota(jnp.int32, (experts * BLOCK, tokens), 0)
    at_short = lax.broadcasted_iota(jnp.int32, (experts * PAD, tokens), 0)
    y_slots = one_hot(at_long == broute_row * BLOCK + bw_row)
    g_slots = one_hot(at_long == broute_row * BLOCK + SLOTS + bw_row)
    x_slots = one_hot((at_long == froute_row * BLOCK + 2 * SLOTS + fw_row) & (fw_row < 8))
    scaled = (row_and_column(bgate[...]) * cot[...].astype(jnp.float32)).astype(jnp.bfloat16)
    for half in range(2):
        at = pl.ds(half * middle, middle)
        placed_b[half] = (
            (
                matmul(y_slots, btok[:, at])
                + matmul(g_slots, scaled[:, half * middle : (half + 1) * middle])
                + matmul(x_slots, ftok[:, at])
            )
            .astype(jnp.bfloat16)
            .reshape(experts, BLOCK, middle)
        )
        all_b[half, c, q, h] = placed_b[half, h]
    tail = jnp.zeros((experts * PAD, quarter), jnp.float32)
    for part in range(4):
        slots = one_hot((at_short == froute_row * PAD + 4 * part + fw_row - 8) & (fw_row >= 8))
        tail = tail + matmul(slots, ftok[:, pl.ds(part * quarter, quarter)])
    placed_f[...] = tail.astype(jnp.bfloat16).reshape(experts, PAD, quarter)
    all_f[c, q, h] = placed_f[h]

    pl.semaphore_wait(barrier, len(others))

    streams = (
        (placed_b.at[0], all_b.at[0]),
        (placed_b.at[1], all_b.at[1]),
        (placed_f, all_f),
    )

    def origin(k):
        return (h + experts - k) % experts

    def cross_send(s):
        placed, alls = streams[s]
        for k in range(1, experts):
            send(
                placed.at[(h + k) % experts],
                alls.at[c, q, h],
                cross_s.at[s, k],
                cross_r.at[s, k],
                crosses[k],
            )

    def spread(s, k, kind, part, dev):
        slot = streams[s][1].at[part[0], part[1], origin(k)]
        send(slot, slot, disp_s.at[s, k, kind], disp_r.at[s, k, kind], dev)

    def arrive(s, k, kind, part, dev):
        slot = streams[s][1].at[part[0], part[1], origin(k)]
        rc(slot, slot, disp_s.at[s, k, kind], disp_r.at[s, k, kind], dev).wait_recv()

    def direct(s, k):
        if k > 0:
            slot = streams[s][1].at[c, q, origin(k)]
            rc(slot, slot, cross_s.at[s, k], cross_r.at[s, k], crosses[k]).wait_recv()
        spread(s, k, 0, (c, q), xn)
        spread(s, k, 1, (c, q), zn)
        spread(s, k, 2, (c, q), sib)

    def forward(s, k):
        arrive(s, k, 0, (c, qx), xn)
        if k % 2 == 0:
            spread(s, k, 5, (c, qx), zn)
        spread(s, k, 3, (c, qx), sib)
        arrive(s, k, 1, (c, qz), zn)
        if k % 2 == 1:
            spread(s, k, 5, (c, qz), xn)
        spread(s, k, 4, (c, qz), sib)

    def last(s, k):
        arrive(s, k, 5, (c, qd), zn if k % 2 == 0 else xn)
        spread(s, k, 6, (c, qd), sib)

    def complete(s, k):
        arrive(s, k, 2, (o, q), sib)
        arrive(s, k, 3, (o, qx), sib)
        arrive(s, k, 4, (o, qz), sib)
        arrive(s, k, 6, (o, qd), sib)

    quarters = (q, qx, qz, qd)

    def mirror_copy(k, at):
        j, own = origin(k), quarters[at]
        return (
            all_b.at[1 - side, c, own, j],
            mirrored.at[c, own, j],
            pipe_s.at[k, at],
            pipe_r.at[k, at],
            mirror,
        )

    def mirror_send(k, at):
        send(*mirror_copy(k, at))

    def mirror_arrive(k, at):
        rc(*mirror_copy(k, at)).wait_recv()
        slot = mirrored.at[c, quarters[at], origin(k)]
        send(slot, slot, side_s.at[k, at], side_r.at[k, at], sib)

    def mirror_complete(k, at):
        slot = mirrored.at[o, quarters[at], origin(k)]
        rc(slot, slot, side_s.at[k, at], side_r.at[k, at], sib).wait_recv()

    later = range(1, experts)
    for s in range(3):
        cross_send(s)
        direct(s, 0)
    mirror_send(0, 0)
    forward(0, 0)
    forward(1, 0)
    mirror_send(0, 1)
    mirror_send(0, 2)
    for k in later:
        direct(0, k)
    last(0, 0)
    last(1, 0)
    mirror_send(0, 3)
    forward(2, 0)
    for k in later:
        direct(1, k)
        mirror_send(k, 0)
        direct(2, k)
    last(2, 0)
    for k in later:
        forward(0, k)
    for k in later:
        forward(1, k)
        mirror_send(k, 1)
        mirror_send(k, 2)
        forward(2, k)
    for k in later:
        for s in range(3):
            last(s, k)
        mirror_send(k, 3)
    for copy in weight_copies:
        copy.wait()
    for k in range(experts):
        for s in range(3):
            complete(s, k)

    def columns(i):
        return pl.ds(pl.multiple_of(i * chunk, chunk), chunk)

    def far_columns(start, i):
        return pl.ds(pl.multiple_of(start + i * chunk, chunk), chunk)

    pre[...] = jnp.zeros_like(pre)
    hgrad[...] = jnp.zeros_like(hgrad)

    def first_step(i, carry):
        for half in range(2):
            at = far_columns(half * middle, i)
            block = all_b[half, :, :, :, :, columns(i)].reshape(long_rows, chunk)
            pre[...] += matmul(block, wgu[at, :])
            hgrad[...] += contract_last(block, wd[:, at])
        return carry

    lax.fori_loop(0, steps, first_step, 0)

    def part_of(value, start):
        return value.reshape(blocks, BLOCK, value.shape[1])[:, start : start + PAD].reshape(
            rows, value.shape[1]
        )

    in_block = lax.broadcasted_iota(jnp.int32, (rows, 1), 0) % PAD
    valid = in_block < SLOTS
    pre_y = part_of(pre[...], 0)
    gate_pre, up_pre = pre_y[:, :hidden], pre_y[:, hidden:]
    hidden_grad = part_of(pltpu.roll(hgrad[...], long_rows - SLOTS, 0), 0)
    sigma = 1.0 / (1.0 + jnp.exp(-gate_pre))
    activated = gate_pre * sigma
    grads[:, 2 * hidden :] = jnp.where(valid, activated * up_pre, 0.0).astype(jnp.bfloat16)
    grads[:, :hidden] = jnp.where(
        valid, hidden_grad * up_pre * sigma * (1.0 + gate_pre * (1.0 - sigma)), 0.0
    ).astype(jnp.bfloat16)
    grads[:, hidden : 2 * hidden] = jnp.where(valid, hidden_grad * activated, 0.0).astype(
        jnp.bfloat16
    )
    send(grads, mgrads, pipe_s.at[0, 4], pipe_r.at[0, 4], mirror)

    def silu_product(value):
        gate, up = value[:, :hidden], value[:, hidden:]
        return gate / (1.0 + jnp.exp(-gate)) * up

    short = all_f[...].reshape(rows, quarter)
    pre_f = matmul(short, wgu[pl.ds(0, quarter), :])
    for part in range(1, 4):
        partial = matmul(short, wgu[pl.ds(part * quarter, quarter), :])
        pre_f = pre_f + pltpu.roll(partial, rows - 4 * part, 0)
    left1[...] = jnp.where(valid, 0.0, pltpu.roll(silu_product(pre_f), SLOTS, 0)).astype(
        jnp.bfloat16
    )
    hid8 = silu_product(part_of(pre[...], PAD))
    left2[:, :hidden] = jnp.where(in_block < 8, pltpu.roll(hid8, rows - 8, 0), 0.0).astype(
        jnp.bfloat16
    )
    left2[:, hidden:] = jnp.where(in_block < 8, 0.0, hid8).astype(jnp.bfloat16)

    def make_parts(s):
        def step(i, carry):
            at = columns(i)
            if s < 2:
                far = far_columns(s * middle, i)
                value = contract_last(grads[:, : 2 * hidden], wgu[far, :])
                value = value + matmul(left1[...], wd[:, far])
            else:
                value = matmul(left2[:, :hidden], wd[:, at])
                value = value + matmul(left2[:, hidden:], wd[:, far_columns(middle, i)])
            parts[s, :, :, :, :, at] = value.astype(jnp.bfloat16).reshape(
                2, 4, experts, PAD, chunk
            )
            return carry

        lax.fori_loop(0, steps, step, 0)
        send(parts.at[s, o], r1.at[s], ret_s.at[s, 0], ret_r.at[s, 0], sib)

    def pass_copy(s, j):
        return (
            parts.at[s, c, qd, j],
            r2a.at[s, j],
            back_s.at[s, j, 0],
            back_r.at[s, j, 0],
            xn if j % 2 == 0 else zn,
        )

    def x_copy(s, j):
        return parts.at[s, c, qx, j], r2x.at[s, j], back_s.at[s, j, 1], back_r.at[s, j, 1], xn

    def z_copy(s, j):
        return parts.at[s, c, qz, j], r2z.at[s, j], back_s.at[s, j, 2], back_r.at[s, j, 2], zn

    def pair_sum(s):
        rc(parts.at[s, o], r1.at[s], ret_s.at[s, 0], ret_r.at[s, 0], sib).wait_recv()

        def add(first):
            parts[s, c, first] = (
                parts[s, c, first].astype(jnp.float32) + r1[s, first].astype(jnp.float32)
            ).astype(jnp.bfloat16)

        add(qd)
        for j in range(experts):
            send(*pass_copy(s, j))
        add(qx)
        for j in range(0, experts, 2):
            send(*x_copy(s, j))
        add(qz)
        for j in range(1, experts, 2):
            send(*z_copy(s, j))
        add(q)

    def passed_on(s):
        for j in range(experts):
            even = j % 2 == 0
            rc(*pass_copy(s, j)).wait_recv()
            to = qz if even else qx
            parts[s, c, to, j] = (
                parts[s, c, to, j].astype(jnp.float32) + r2a[s, j].astype(jnp.float32)
            ).astype(jnp.bfloat16)
            if even:
                send(*z_copy(s, j))
            else:
                send(*x_copy(s, j))

    def summed(s):
        for j in range(experts):
            rc(*x_copy(s, j)).wait_recv()
            rc(*z_copy(s, j)).wait_recv()
            tsend[s, j] = (
                parts[s, c, q, j].astype(jnp.float32)
                + r2x[s, j].astype(jnp.float32)
                + r2z[s, j].astype(jnp.float32)
            ).astype(jnp.bfloat16)
        for k in later:
            send(
                tsend.at[s, (h + k) % experts],
                r3.at[s, h],
                ret_s.at[s, k],
                ret_r.at[s, k],
                crosses[k],
            )
        r3[s, h] = tsend[s, h]

    def home(s):
        for k in later:
            slot = r3.at[s, origin(k)]
            rc(slot, slot, ret_s.at[s, k], ret_r.at[s, k], crosses[k]).wait_recv()
        return r3[s].reshape(experts * PAD, middle)

    def transposed(source, target):
        spaced[:, :PAD] = source[...].reshape(blocks, PAD, 3 * hidden)
        spaced[:, PAD:] = jnp.zeros((blocks, BLOCK - PAD, 3 * hidden), jnp.bfloat16)
        full = spaced[...].reshape(long_rows, 3 * hidden)
        target[: 2 * hidden, :] = full[:, : 2 * hidden].T
        down = pltpu.roll(full[:, 2 * hidden :].astype(jnp.float32), SLOTS, 0)
        target[2 * hidden :, :] = down.astype(jnp.bfloat16).T

    def weight_grads(first, end):
        def step(i, carry):
            at = columns(i)
            block = all_b[side, :, :, :, :, at].reshape(long_rows, chunk)
            far = mirrored[:, :, :, :, at].reshape(long_rows, chunk)
            total = matmul(grads_t[...], block) + matmul(mgrads_t[...], far)
            both = total[: 2 * hidden].T.astype(jnp.bfloat16)
            out_g[at, :] = both[:, :hidden]
            out_u[at, :] = both[:, hidden:]
            out_d[:, at] = total[2 * hidden :].astype(jnp.bfloat16)
            return carry

        lax.fori_loop(first, end, step, 0)

    make_parts(0)
    make_parts(1)
    pair_sum(0)
    make_parts(2)
    pair_sum(1)
    for k in range(experts):
        for at in range(4):
            mirror_arrive(k, at)
    passed_on(0)
    pair_sum(2)
    transposed(grads, grads_t)
    passed_on(1)
    rc(grads, mgrads, pipe_s.at[0, 4], pipe_r.at[0, 4], mirror).wait_recv()
    transposed(mgrads, mgrads_t)
    for k in range(experts):
        for at in range(4):
            mirror_complete(k, at)
    summed(0)
    passed_on(2)
    weight_grads(0, steps // 2)
    summed(1)
    weight_grads(steps // 2, steps)
    summed(2)

    at_t = lax.broadcasted_iota(jnp.int32, (tokens, experts * PAD), 1)
    b_slots = one_hot(at_t == broute_col * PAD + bw_col)
    f_last = one_hot((at_t == froute_col * PAD + fw_col + 4) & (fw_col >= 8))
    f_left = one_hot((at_t == froute_col * PAD + fw_col) & (fw_col < 8))
    f_right = one_hot((at_t == froute_col * PAD + fw_col + 8) & (fw_col < 8))
    fgate_col = row_and_column(fgate[...])
    first = home(0)
    out_b[:, :middle] = matmul(b_slots, first).astype(jnp.bfloat16)
    second = home(1)
    out_b[:, middle:] = matmul(b_slots, second).astype(jnp.bfloat16)
    third = home(2)
    out_f[:, :middle] = (fgate_col * (matmul(f_last, first) + matmul(f_left, third))).astype(
        jnp.bfloat16
    )
    out_f[:, middle:] = (fgate_col * (matmul(f_last, second) + matmul(f_right, third))).astype(
        jnp.bfloat16
    )
    for copy in sent:
        copy.wait_send()


def hand_out(*refs):
    sources, targets, held, sems = refs[:5], refs[5:10], refs[10:15], refs[15]
    reads = [pltpu.make_async_copy(sources[i], held[i], sems.at[0, i]) for i in range(5)]
    writes = [pltpu.make_async_copy(held[i], targets[i], sems.at[1, i]) for i in range(5)]
    for read in reads:
        read.start()
    for read, write in zip(reads, writes):
        read.wait()
        write.start()
    for write in writes:
        write.wait()


def on_device(
    forward_tokens,
    forward_routing,
    forward_gates,
    backward_tokens,
    backward_routing,
    backward_gates,
    cotangent,
    gate_matrix,
    up_matrix,
    down_matrix,
):
    devices = lax.axis_size("expert")
    positions = lax.axis_size("pipe")
    experts = devices // SHARING_CARDS
    tokens, width = forward_tokens.shape[1:]
    hidden = gate_matrix.shape[2]
    middle = width // 2
    blocks = SHARING_CARDS * experts
    rows = blocks * PAD
    assert max(tokens // 3, tokens // experts) <= SLOTS
    bf16, f32 = jnp.bfloat16, jnp.float32
    vmem = pl.BlockSpec(memory_space=pltpu.VMEM)
    far = pl.BlockSpec(memory_space=pl.ANY)
    dma = pltpu.SemaphoreType.DMA
    outs = pl.pallas_call(
        functools.partial(kernel, experts, positions),
        out_shape=(
            jax.ShapeDtypeStruct((tokens, width), bf16),
            jax.ShapeDtypeStruct((tokens, width), bf16),
            jax.ShapeDtypeStruct((middle, hidden), bf16),
            jax.ShapeDtypeStruct((middle, hidden), bf16),
            jax.ShapeDtypeStruct((hidden, middle), bf16),
        ),
        in_specs=[vmem] * 7 + [far] * 3,
        out_specs=(vmem,) * 5,
        scratch_shapes=[
            pltpu.VMEM((width, 2 * hidden), bf16),
            pltpu.VMEM((hidden, width), bf16),
            pltpu.VMEM((2, experts, BLOCK, middle), bf16),
            pltpu.VMEM((experts, PAD, width // 4), bf16),
            pltpu.VMEM((2, 2, 4, experts, BLOCK, middle), bf16),
            pltpu.VMEM((2, 4, experts, PAD, width // 4), bf16),
            pltpu.VMEM((3, 2, 4, experts, PAD, middle), bf16),
            pltpu.VMEM((3, 4, experts, PAD, middle), bf16),
            pltpu.VMEM((3, experts, PAD, middle), bf16),
            pltpu.VMEM((3, experts, PAD, middle), bf16),
            pltpu.VMEM((3, experts, PAD, middle), bf16),
            pltpu.VMEM((3, experts, PAD, middle), bf16),
            pltpu.VMEM((3, experts, PAD, middle), bf16),
            pltpu.VMEM((blocks * BLOCK, 2 * hidden), f32),
            pltpu.VMEM((blocks * BLOCK, hidden), f32),
            pltpu.VMEM((rows, 3 * hidden), bf16),
            pltpu.VMEM((rows, 3 * hidden), bf16),
            pltpu.VMEM((blocks, BLOCK, 3 * hidden), bf16),
            pltpu.VMEM((3 * hidden, blocks * BLOCK), bf16),
            pltpu.VMEM((3 * hidden, blocks * BLOCK), bf16),
            pltpu.VMEM((rows, hidden), bf16),
            pltpu.VMEM((rows, 2 * hidden), bf16),
            pltpu.VMEM((2, 4, experts, BLOCK, middle), bf16),
            dma((3,)),
            dma((3, experts)),
            dma((3, experts)),
            dma((3, experts, 7)),
            dma((3, experts, 7)),
            dma((3, experts)),
            dma((3, experts)),
            dma((3, experts, 3)),
            dma((3, experts, 3)),
            dma((experts, 5)),
            dma((experts, 5)),
            dma((experts, 4)),
            dma((experts, 4)),
        ],
        compiler_params=pltpu.CompilerParams(
            collective_id=0, has_side_effects=True, vmem_limit_bytes=60 * 1024 * 1024
        ),
    )(
        forward_tokens[0],
        forward_routing.reshape(1, tokens),
        forward_gates,
        backward_tokens[0],
        backward_routing.reshape(1, tokens),
        backward_gates,
        cotangent[0],
        gate_matrix[0],
        up_matrix[0],
        down_matrix[0],
    )
    outs = pl.pallas_call(
        hand_out,
        out_shape=tuple(jax.ShapeDtypeStruct(out.shape, bf16) for out in outs),
        in_specs=[pl.BlockSpec(memory_space=pl.ANY)] * 5,
        out_specs=(pl.BlockSpec(memory_space=pl.ANY),) * 5,
        scratch_shapes=[pltpu.VMEM(out.shape, bf16) for out in outs] + [dma((2, 5))],
        compiler_params=pltpu.CompilerParams(vmem_limit_bytes=60 * 1024 * 1024),
    )(*outs)
    return tuple(out[None] for out in outs)


def solution(mesh):
    in_specs = (
        P("pipe", "expert", None),
        P("pipe", "expert", None),
        P("pipe", "expert"),
        P("pipe", "expert", None),
        P("pipe", "expert", None),
        P("pipe", "expert"),
        P("pipe", "expert", None),
        P("pipe", None, "expert"),
        P("pipe", None, "expert"),
        P("pipe", "expert", None),
    )
    out_specs = (
        P("pipe", "expert", None),
        P("pipe", "expert", None),
        P("pipe", None, "expert"),
        P("pipe", None, "expert"),
        P("pipe", "expert", None),
    )
    return jax.shard_map(
        on_device, mesh=mesh, in_specs=in_specs, out_specs=out_specs, check_vma=False
    )
```

```python
import functools

import jax
import jax.numpy as jnp
from jax import lax
from jax.experimental import pallas as pl
from jax.experimental.pallas import tpu as pltpu
from jax.sharding import PartitionSpec as P

SHARING_CARDS = 8
PAD = 16
SLOTS = 12
BLOCK = 32
MESH = pl.DeviceIdType.MESH


def flip(value, bit):
    return value + bit - 2 * bit * ((value // bit) % 2)


def contract_last(left, right):
    return lax.dot_general(
        left, right, (((1,), (1,)), ((), ())), preferred_element_type=jnp.float32
    )


def matmul(left, right):
    return jnp.dot(left, right, preferred_element_type=jnp.float32)


def row_and_column(row):
    n = row.shape[1]
    at0 = lax.broadcasted_iota(jnp.int32, (n, n), 0)
    at1 = lax.broadcasted_iota(jnp.int32, (n, n), 1)
    return jnp.sum(jnp.where(at0 == at1, row, jnp.zeros_like(row)), axis=1, keepdims=True)


def within(routing_row):
    n = routing_row.shape[1]
    column = row_and_column(routing_row)
    at0 = lax.broadcasted_iota(jnp.int32, (n, n), 0)
    at1 = lax.broadcasted_iota(jnp.int32, (n, n), 1)
    same = column == routing_row
    before_row = jnp.sum(jnp.where(same & (at0 < at1), 1.0, 0.0), axis=0, keepdims=True)
    before_column = jnp.sum(jnp.where(same & (at1 < at0), 1.0, 0.0), axis=1, keepdims=True)
    return before_row.astype(jnp.int32), column, before_column.astype(jnp.int32)


def one_hot(condition):
    return jnp.where(condition, 1.0, 0.0).astype(jnp.bfloat16)


def kernel(
    experts,
    positions,
    ftok,
    froute,
    fgate,
    btok,
    broute,
    bgate,
    cot,
    wg,
    wu,
    wd_far,
    out_f,
    out_b,
    out_g,
    out_u,
    out_d,
    wgu,
    wd,
    placed_b,
    placed_f,
    all_b,
    all_f,
    parts,
    r1,
    r2a,
    r2x,
    r2z,
    tsend,
    r3,
    pre,
    hgrad,
    grads,
    mgrads,
    spaced,
    grads_t,
    mgrads_t,
    left1,
    left2,
    mirrored,
    weight_s,
    cross_s,
    cross_r,
    disp_s,
    disp_r,
    ret_s,
    ret_r,
    back_s,
    back_r,
    pipe_s,
    pipe_r,
    side_s,
    side_r,
):
    tokens, width = ftok.shape
    hidden = wg.shape[1]
    middle = width // 2
    quarter = width // 4
    chunk = 256
    steps = middle // chunk
    blocks = SHARING_CARDS * experts
    rows = blocks * PAD
    long_rows = blocks * BLOCK
    e = lax.axis_index("expert")
    p = lax.axis_index("pipe")
    h = e // SHARING_CARDS
    m = e % SHARING_CARDS
    base = h * SHARING_CARDS
    c = m % 2
    o = 1 - c
    q = m // 2
    qx, qz = flip(q, 1), flip(q, 2)
    qd = flip(qx, 2)
    sib = {"expert": base + flip(m, 1)}
    xn = {"expert": base + flip(m, 2)}
    zn = {"expert": base + flip(m, 4)}
    mirror = {"pipe": positions - 1 - p}
    side = p // (positions // 2)
    crosses = [{"expert": ((h + k) % experts) * SHARING_CARDS + m} for k in range(experts)]

    barrier = pltpu.get_barrier_semaphore()
    others = [sib, xn, zn, mirror] + crosses[1:]
    for other in others:
        pl.semaphore_signal(barrier, inc=1, device_id=other, device_id_type=MESH)

    weight_copies = [
        pltpu.make_async_copy(wg, wgu.at[:, pl.ds(0, hidden)], weight_s.at[0]),
        pltpu.make_async_copy(wu, wgu.at[:, pl.ds(hidden, hidden)], weight_s.at[1]),
        pltpu.make_async_copy(wd_far, wd, weight_s.at[2]),
    ]
    for copy in weight_copies:
        copy.start()

    def rc(src, dst, ss, rs, dev):
        return pltpu.make_async_remote_copy(
            src_ref=src, dst_ref=dst, send_sem=ss, recv_sem=rs, device_id=dev, device_id_type=MESH
        )

    sent = []

    def send(src, dst, ss, rs, dev):
        copy = rc(src, dst, ss, rs, dev)
        copy.start()
        sent.append(copy)

    broute_row, froute_row = broute[...], froute[...]
    bw_row, broute_col, bw_col = within(broute_row)
    fw_row, froute_col, fw_col = within(froute_row)
    at_long = lax.broadcasted_iota(jnp.int32, (experts * BLOCK, tokens), 0)
    at_short = lax.broadcasted_iota(jnp.int32, (experts * PAD, tokens), 0)
    y_slots = one_hot(at_long == broute_row * BLOCK + bw_row)
    g_slots = one_hot(at_long == broute_row * BLOCK + SLOTS + bw_row)
    x_slots = one_hot((at_long == froute_row * BLOCK + 2 * SLOTS + fw_row) & (fw_row < 8))
    scaled = (row_and_column(bgate[...]) * cot[...].astype(jnp.float32)).astype(jnp.bfloat16)
    for half in range(2):
        at = pl.ds(half * middle, middle)
        placed_b[half] = (
            (
                matmul(y_slots, btok[:, at])
                + matmul(g_slots, scaled[:, half * middle : (half + 1) * middle])
                + matmul(x_slots, ftok[:, at])
            )
            .astype(jnp.bfloat16)
            .reshape(experts, BLOCK, middle)
        )
        all_b[half, c, q, h] = placed_b[half, h]
    tail = jnp.zeros((experts * PAD, quarter), jnp.float32)
    for part in range(4):
        slots = one_hot((at_short == froute_row * PAD + 4 * part + fw_row - 8) & (fw_row >= 8))
        tail = tail + matmul(slots, ftok[:, pl.ds(part * quarter, quarter)])
    placed_f[...] = tail.astype(jnp.bfloat16).reshape(experts, PAD, quarter)
    all_f[c, q, h] = placed_f[h]

    pl.semaphore_wait(barrier, len(others))

    streams = (
        (placed_b.at[0], all_b.at[0]),
        (placed_b.at[1], all_b.at[1]),
        (placed_f, all_f),
    )

    def origin(k):
        return (h + experts - k) % experts

    def cross_send(s):
        placed, alls = streams[s]
        for k in range(1, experts):
            send(
                placed.at[(h + k) % experts],
                alls.at[c, q, h],
                cross_s.at[s, k],
                cross_r.at[s, k],
                crosses[k],
            )

    def spread(s, k, kind, part, dev):
        slot = streams[s][1].at[part[0], part[1], origin(k)]
        send(slot, slot, disp_s.at[s, k, kind], disp_r.at[s, k, kind], dev)

    def arrive(s, k, kind, part, dev):
        slot = streams[s][1].at[part[0], part[1], origin(k)]
        rc(slot, slot, disp_s.at[s, k, kind], disp_r.at[s, k, kind], dev).wait_recv()

    def direct(s, k):
        if k > 0:
            slot = streams[s][1].at[c, q, origin(k)]
            rc(slot, slot, cross_s.at[s, k], cross_r.at[s, k], crosses[k]).wait_recv()
        spread(s, k, 0, (c, q), xn)
        spread(s, k, 1, (c, q), zn)
        spread(s, k, 2, (c, q), sib)

    def by_z(s, k):
        return k % 2 == 0 and s == 0

    def forward(s, k):
        arrive(s, k, 0, (c, qx), xn)
        if by_z(s, k):
            spread(s, k, 5, (c, qx), zn)
        spread(s, k, 3, (c, qx), sib)
        arrive(s, k, 1, (c, qz), zn)
        if not by_z(s, k):
            spread(s, k, 5, (c, qz), xn)
        spread(s, k, 4, (c, qz), sib)

    def last(s, k):
        arrive(s, k, 5, (c, qd), zn if by_z(s, k) else xn)
        spread(s, k, 6, (c, qd), sib)

    def complete(s, k):
        arrive(s, k, 2, (o, q), sib)
        arrive(s, k, 3, (o, qx), sib)
        arrive(s, k, 4, (o, qz), sib)
        arrive(s, k, 6, (o, qd), sib)

    quarters = (q, qx, qz, qd)

    def mirror_copy(k, at):
        j, own = origin(k), quarters[at]
        return (
            all_b.at[1 - side, c, own, j],
            mirrored.at[c, own, j],
            pipe_s.at[k, at],
            pipe_r.at[k, at],
            mirror,
        )

    def mirror_send(k, at):
        send(*mirror_copy(k, at))

    def mirror_arrive(k, at):
        rc(*mirror_copy(k, at)).wait_recv()
        slot = mirrored.at[c, quarters[at], origin(k)]
        send(slot, slot, side_s.at[k, at], side_r.at[k, at], sib)

    def mirror_complete(k, at):
        slot = mirrored.at[o, quarters[at], origin(k)]
        rc(slot, slot, side_s.at[k, at], side_r.at[k, at], sib).wait_recv()

    def columns(i):
        return pl.ds(pl.multiple_of(i * chunk, chunk), chunk)

    def far_columns(start, i):
        return pl.ds(pl.multiple_of(start + i * chunk, chunk), chunk)

    def first_products(k, half):
        j = origin(k)

        def step(i, carry):
            at = far_columns(half * middle, i)
            block = all_b[half, :, :, j, :, columns(i)].reshape(SHARING_CARDS * BLOCK, chunk)
            both = matmul(block, wgu[at, :]).reshape(SHARING_CARDS, BLOCK, 2 * hidden)
            down = contract_last(block, wd[:, at]).reshape(SHARING_CARDS, BLOCK, hidden)
            pre[:, j] += both
            hgrad[:, j] += down
            return carry

        lax.fori_loop(0, steps, step, 0)

    later = range(1, experts)
    for s in range(3):
        cross_send(s)
        direct(s, 0)
    mirror_send(0, 0)
    pre[...] = jnp.zeros_like(pre)
    hgrad[...] = jnp.zeros_like(hgrad)
    forward(0, 0)
    forward(1, 0)
    mirror_send(0, 1)
    mirror_send(0, 2)
    for k in later:
        direct(0, k)
    last(0, 0)
    last(1, 0)
    mirror_send(0, 3)
    forward(2, 0)
    for k in later:
        direct(1, k)
        mirror_send(k, 0)
        direct(2, k)
    last(2, 0)
    for copy in weight_copies:
        copy.wait()
    complete(0, 0)
    first_products(0, 0)
    for k in later:
        forward(0, k)
    complete(1, 0)
    first_products(0, 1)
    for k in later:
        forward(1, k)
        mirror_send(k, 1)
        mirror_send(k, 2)
        forward(2, k)
    for k in later:
        for s in range(3):
            last(s, k)
        mirror_send(k, 3)
    for k in later:
        complete(0, k)
        first_products(k, 0)
    for k in later:
        complete(1, k)
        first_products(k, 1)
    for k in range(experts):
        complete(2, k)

    def part_of(value, start):
        return value.reshape(blocks, BLOCK, value.shape[1])[:, start : start + PAD].reshape(
            rows, value.shape[1]
        )

    in_block = lax.broadcasted_iota(jnp.int32, (rows, 1), 0) % PAD
    valid = in_block < SLOTS
    pre_all = pre[...].reshape(long_rows, 2 * hidden)
    hgrad_all = hgrad[...].reshape(long_rows, hidden)
    pre_y = part_of(pre_all, 0)
    gate_pre, up_pre = pre_y[:, :hidden], pre_y[:, hidden:]
    hidden_grad = part_of(pltpu.roll(hgrad_all, long_rows - SLOTS, 0), 0)
    sigma = 1.0 / (1.0 + jnp.exp(-gate_pre))
    activated = gate_pre * sigma
    grads[:, 2 * hidden :] = jnp.where(valid, activated * up_pre, 0.0).astype(jnp.bfloat16)
    grads[:, :hidden] = jnp.where(
        valid, hidden_grad * up_pre * sigma * (1.0 + gate_pre * (1.0 - sigma)), 0.0
    ).astype(jnp.bfloat16)
    grads[:, hidden : 2 * hidden] = jnp.where(valid, hidden_grad * activated, 0.0).astype(
        jnp.bfloat16
    )
    send(grads, mgrads, pipe_s.at[0, 4], pipe_r.at[0, 4], mirror)

    def silu_product(value):
        gate, up = value[:, :hidden], value[:, hidden:]
        return gate / (1.0 + jnp.exp(-gate)) * up

    short = all_f[...].reshape(rows, quarter)
    pre_f = matmul(short, wgu[pl.ds(0, quarter), :])
    for part in range(1, 4):
        partial = matmul(short, wgu[pl.ds(part * quarter, quarter), :])
        pre_f = pre_f + pltpu.roll(partial, rows - 4 * part, 0)
    left1[...] = jnp.where(valid, 0.0, pltpu.roll(silu_product(pre_f), SLOTS, 0)).astype(
        jnp.bfloat16
    )
    hid8 = silu_product(part_of(pre_all, PAD))
    left2[:, :hidden] = jnp.where(in_block < 8, pltpu.roll(hid8, rows - 8, 0), 0.0).astype(
        jnp.bfloat16
    )
    left2[:, hidden:] = jnp.where(in_block < 8, 0.0, hid8).astype(jnp.bfloat16)

    def make_parts(s):
        def step(i, carry):
            at = columns(i)
            if s < 2:
                far = far_columns(s * middle, i)
                value = contract_last(grads[:, : 2 * hidden], wgu[far, :])
                value = value + matmul(left1[...], wd[:, far])
            else:
                value = matmul(left2[:, :hidden], wd[:, at])
                value = value + matmul(left2[:, hidden:], wd[:, far_columns(middle, i)])
            parts[s, :, :, :, :, at] = value.astype(jnp.bfloat16).reshape(
                2, 4, experts, PAD, chunk
            )
            return carry

        lax.fori_loop(0, steps, step, 0)
        send(parts.at[s, o], r1.at[s], ret_s.at[s, 0], ret_r.at[s, 0], sib)

    def x_first(s, j):
        return j % 2 == 0 or s > 0

    def pass_copy(s, j):
        return (
            parts.at[s, c, qd, j],
            r2a.at[s, j],
            back_s.at[s, j, 0],
            back_r.at[s, j, 0],
            xn if x_first(s, j) else zn,
        )

    def x_copy(s, j):
        return parts.at[s, c, qx, j], r2x.at[s, j], back_s.at[s, j, 1], back_r.at[s, j, 1], xn

    def z_copy(s, j):
        return parts.at[s, c, qz, j], r2z.at[s, j], back_s.at[s, j, 2], back_r.at[s, j, 2], zn

    def pair_sum(s):
        rc(parts.at[s, o], r1.at[s], ret_s.at[s, 0], ret_r.at[s, 0], sib).wait_recv()

        def add(first):
            parts[s, c, first] = (
                parts[s, c, first].astype(jnp.float32) + r1[s, first].astype(jnp.float32)
            ).astype(jnp.bfloat16)

        add(qd)
        for j in range(experts):
            send(*pass_copy(s, j))
        add(qx)
        for j in range(experts):
            if x_first(s, j):
                send(*x_copy(s, j))
        add(qz)
        for j in range(experts):
            if not x_first(s, j):
                send(*z_copy(s, j))
        add(q)

    def passed_on(s):
        for j in range(experts):
            rc(*pass_copy(s, j)).wait_recv()
            to = qz if x_first(s, j) else qx
            parts[s, c, to, j] = (
                parts[s, c, to, j].astype(jnp.float32) + r2a[s, j].astype(jnp.float32)
            ).astype(jnp.bfloat16)
            if x_first(s, j):
                send(*z_copy(s, j))
            else:
                send(*x_copy(s, j))

    def summed(s):
        for j in range(experts):
            rc(*x_copy(s, j)).wait_recv()
            rc(*z_copy(s, j)).wait_recv()
            tsend[s, j] = (
                parts[s, c, q, j].astype(jnp.float32)
                + r2x[s, j].astype(jnp.float32)
                + r2z[s, j].astype(jnp.float32)
            ).astype(jnp.bfloat16)
        for k in later:
            send(
                tsend.at[s, (h + k) % experts],
                r3.at[s, h],
                ret_s.at[s, k],
                ret_r.at[s, k],
                crosses[k],
            )
        r3[s, h] = tsend[s, h]

    def home(s):
        for k in later:
            slot = r3.at[s, origin(k)]
            rc(slot, slot, ret_s.at[s, k], ret_r.at[s, k], crosses[k]).wait_recv()
        return r3[s].reshape(experts * PAD, middle)

    def transposed(source, target):
        spaced[:, :PAD] = source[...].reshape(blocks, PAD, 3 * hidden)
        spaced[:, PAD:] = jnp.zeros((blocks, BLOCK - PAD, 3 * hidden), jnp.bfloat16)
        full = spaced[...].reshape(long_rows, 3 * hidden)
        target[: 2 * hidden, :] = full[:, : 2 * hidden].T
        down = pltpu.roll(full[:, 2 * hidden :].astype(jnp.float32), SLOTS, 0)
        target[2 * hidden :, :] = down.astype(jnp.bfloat16).T

    def weight_grads(first, end):
        def step(i, carry):
            at = columns(i)
            block = all_b[side, :, :, :, :, at].reshape(long_rows, chunk)
            far = mirrored[:, :, :, :, at].reshape(long_rows, chunk)
            total = matmul(grads_t[...], block) + matmul(mgrads_t[...], far)
            both = total[: 2 * hidden].T.astype(jnp.bfloat16)
            out_g[at, :] = both[:, :hidden]
            out_u[at, :] = both[:, hidden:]
            out_d[:, at] = total[2 * hidden :].astype(jnp.bfloat16)
            return carry

        lax.fori_loop(first, end, step, 0)

    make_parts(0)
    make_parts(1)
    pair_sum(0)
    make_parts(2)
    pair_sum(1)
    for k in range(experts):
        for at in range(4):
            mirror_arrive(k, at)
    passed_on(0)
    pair_sum(2)
    transposed(grads, grads_t)
    passed_on(1)
    rc(grads, mgrads, pipe_s.at[0, 4], pipe_r.at[0, 4], mirror).wait_recv()
    transposed(mgrads, mgrads_t)
    for k in range(experts):
        for at in range(4):
            mirror_complete(k, at)
    summed(0)
    passed_on(2)
    weight_grads(0, steps // 3)
    summed(1)
    weight_grads(steps // 3, 2 * steps // 3)
    summed(2)
    weight_grads(2 * steps // 3, steps)

    at_t = lax.broadcasted_iota(jnp.int32, (tokens, experts * PAD), 1)
    b_slots = one_hot(at_t == broute_col * PAD + bw_col)
    f_last = one_hot((at_t == froute_col * PAD + fw_col + 4) & (fw_col >= 8))
    f_left = one_hot((at_t == froute_col * PAD + fw_col) & (fw_col < 8))
    f_right = one_hot((at_t == froute_col * PAD + fw_col + 8) & (fw_col < 8))
    fgate_col = row_and_column(fgate[...])
    first = home(0)
    out_b[:, :middle] = matmul(b_slots, first).astype(jnp.bfloat16)
    second = home(1)
    out_b[:, middle:] = matmul(b_slots, second).astype(jnp.bfloat16)
    third = home(2)
    out_f[:, :middle] = (fgate_col * (matmul(f_last, first) + matmul(f_left, third))).astype(
        jnp.bfloat16
    )
    out_f[:, middle:] = (fgate_col * (matmul(f_last, second) + matmul(f_right, third))).astype(
        jnp.bfloat16
    )
    for copy in sent:
        copy.wait_send()


def hand_out(*refs):
    sources, targets, held, sems = refs[:5], refs[5:10], refs[10:15], refs[15]
    reads = [pltpu.make_async_copy(sources[i], held[i], sems.at[0, i]) for i in range(5)]
    writes = [pltpu.make_async_copy(held[i], targets[i], sems.at[1, i]) for i in range(5)]
    for read in reads:
        read.start()
    for read, write in zip(reads, writes):
        read.wait()
        write.start()
    for write in writes:
        write.wait()


def on_device(
    forward_tokens,
    forward_routing,
    forward_gates,
    backward_tokens,
    backward_routing,
    backward_gates,
    cotangent,
    gate_matrix,
    up_matrix,
    down_matrix,
):
    devices = lax.axis_size("expert")
    positions = lax.axis_size("pipe")
    experts = devices // SHARING_CARDS
    tokens, width = forward_tokens.shape[1:]
    hidden = gate_matrix.shape[2]
    middle = width // 2
    blocks = SHARING_CARDS * experts
    rows = blocks * PAD
    assert max(tokens // 3, tokens // experts) <= SLOTS
    bf16, f32 = jnp.bfloat16, jnp.float32
    vmem = pl.BlockSpec(memory_space=pltpu.VMEM)
    far = pl.BlockSpec(memory_space=pl.ANY)
    dma = pltpu.SemaphoreType.DMA
    outs = pl.pallas_call(
        functools.partial(kernel, experts, positions),
        out_shape=(
            jax.ShapeDtypeStruct((tokens, width), bf16),
            jax.ShapeDtypeStruct((tokens, width), bf16),
            jax.ShapeDtypeStruct((middle, hidden), bf16),
            jax.ShapeDtypeStruct((middle, hidden), bf16),
            jax.ShapeDtypeStruct((hidden, middle), bf16),
        ),
        in_specs=[vmem] * 7 + [far] * 3,
        out_specs=(vmem,) * 5,
        scratch_shapes=[
            pltpu.VMEM((width, 2 * hidden), bf16),
            pltpu.VMEM((hidden, width), bf16),
            pltpu.VMEM((2, experts, BLOCK, middle), bf16),
            pltpu.VMEM((experts, PAD, width // 4), bf16),
            pltpu.VMEM((2, 2, 4, experts, BLOCK, middle), bf16),
            pltpu.VMEM((2, 4, experts, PAD, width // 4), bf16),
            pltpu.VMEM((3, 2, 4, experts, PAD, middle), bf16),
            pltpu.VMEM((3, 4, experts, PAD, middle), bf16),
            pltpu.VMEM((3, experts, PAD, middle), bf16),
            pltpu.VMEM((3, experts, PAD, middle), bf16),
            pltpu.VMEM((3, experts, PAD, middle), bf16),
            pltpu.VMEM((3, experts, PAD, middle), bf16),
            pltpu.VMEM((3, experts, PAD, middle), bf16),
            pltpu.VMEM((SHARING_CARDS, experts, BLOCK, 2 * hidden), f32),
            pltpu.VMEM((SHARING_CARDS, experts, BLOCK, hidden), f32),
            pltpu.VMEM((rows, 3 * hidden), bf16),
            pltpu.VMEM((rows, 3 * hidden), bf16),
            pltpu.VMEM((blocks, BLOCK, 3 * hidden), bf16),
            pltpu.VMEM((3 * hidden, blocks * BLOCK), bf16),
            pltpu.VMEM((3 * hidden, blocks * BLOCK), bf16),
            pltpu.VMEM((rows, hidden), bf16),
            pltpu.VMEM((rows, 2 * hidden), bf16),
            pltpu.VMEM((2, 4, experts, BLOCK, middle), bf16),
            dma((3,)),
            dma((3, experts)),
            dma((3, experts)),
            dma((3, experts, 7)),
            dma((3, experts, 7)),
            dma((3, experts)),
            dma((3, experts)),
            dma((3, experts, 3)),
            dma((3, experts, 3)),
            dma((experts, 5)),
            dma((experts, 5)),
            dma((experts, 4)),
            dma((experts, 4)),
        ],
        compiler_params=pltpu.CompilerParams(
            collective_id=0, has_side_effects=True, vmem_limit_bytes=60 * 1024 * 1024
        ),
    )(
        forward_tokens[0],
        forward_routing.reshape(1, tokens),
        forward_gates,
        backward_tokens[0],
        backward_routing.reshape(1, tokens),
        backward_gates,
        cotangent[0],
        gate_matrix[0],
        up_matrix[0],
        down_matrix[0],
    )
    outs = pl.pallas_call(
        hand_out,
        out_shape=tuple(jax.ShapeDtypeStruct(out.shape, bf16) for out in outs),
        in_specs=[pl.BlockSpec(memory_space=pl.ANY)] * 5,
        out_specs=(pl.BlockSpec(memory_space=pl.ANY),) * 5,
        scratch_shapes=[pltpu.VMEM(out.shape, bf16) for out in outs] + [dma((2, 5))],
        compiler_params=pltpu.CompilerParams(vmem_limit_bytes=60 * 1024 * 1024),
    )(*outs)
    return tuple(out[None] for out in outs)


def solution(mesh):
    in_specs = (
        P("pipe", "expert", None),
        P("pipe", "expert", None),
        P("pipe", "expert"),
        P("pipe", "expert", None),
        P("pipe", "expert", None),
        P("pipe", "expert"),
        P("pipe", "expert", None),
        P("pipe", None, "expert"),
        P("pipe", None, "expert"),
        P("pipe", "expert", None),
    )
    out_specs = (
        P("pipe", "expert", None),
        P("pipe", "expert", None),
        P("pipe", None, "expert"),
        P("pipe", None, "expert"),
        P("pipe", "expert", None),
    )
    return jax.shard_map(
        on_device, mesh=mesh, in_specs=in_specs, out_specs=out_specs, check_vma=False
    )
```

```python
import functools

import jax
import jax.numpy as jnp
from jax import lax
from jax.experimental import pallas as pl
from jax.experimental.pallas import tpu as pltpu
from jax.sharding import PartitionSpec as P

SHARING_CARDS = 8
PAD = 16
SLOTS = 12
BLOCK = 32
MESH = pl.DeviceIdType.MESH


def flip(value, bit):
    return value + bit - 2 * bit * ((value // bit) % 2)


def contract_last(left, right):
    return lax.dot_general(
        left, right, (((1,), (1,)), ((), ())), preferred_element_type=jnp.float32
    )


def matmul(left, right):
    return jnp.dot(left, right, preferred_element_type=jnp.float32)


def row_and_column(row):
    n = row.shape[1]
    at0 = lax.broadcasted_iota(jnp.int32, (n, n), 0)
    at1 = lax.broadcasted_iota(jnp.int32, (n, n), 1)
    return jnp.sum(jnp.where(at0 == at1, row, jnp.zeros_like(row)), axis=1, keepdims=True)


def within(routing_row):
    n = routing_row.shape[1]
    column = row_and_column(routing_row)
    at0 = lax.broadcasted_iota(jnp.int32, (n, n), 0)
    at1 = lax.broadcasted_iota(jnp.int32, (n, n), 1)
    same = column == routing_row
    before_row = jnp.sum(jnp.where(same & (at0 < at1), 1.0, 0.0), axis=0, keepdims=True)
    before_column = jnp.sum(jnp.where(same & (at1 < at0), 1.0, 0.0), axis=1, keepdims=True)
    return before_row.astype(jnp.int32), column, before_column.astype(jnp.int32)


def one_hot(condition):
    return jnp.where(condition, 1.0, 0.0).astype(jnp.bfloat16)


def kernel(
    experts,
    positions,
    ftok,
    froute,
    fgate,
    btok,
    broute,
    bgate,
    cot,
    wg,
    wu,
    wd_far,
    out_f,
    out_b,
    far_g,
    far_u,
    far_d,
    out_g,
    out_u,
    out_d,
    wgu,
    wd,
    placed_b,
    placed_f,
    all_b,
    all_f,
    parts,
    r1,
    r2a,
    r2x,
    r2z,
    tsend,
    r3,
    pre,
    hgrad,
    grads,
    mgrads,
    spaced,
    grads_t,
    mgrads_t,
    left1,
    left2,
    mirrored,
    weight_s,
    out_s,
    cross_s,
    cross_r,
    disp_s,
    disp_r,
    ret_s,
    ret_r,
    back_s,
    back_r,
    pipe_s,
    pipe_r,
    side_s,
    side_r,
):
    tokens, width = ftok.shape
    hidden = wg.shape[1]
    middle = width // 2
    quarter = width // 4
    chunk = 256
    steps = middle // chunk
    blocks = SHARING_CARDS * experts
    rows = blocks * PAD
    long_rows = blocks * BLOCK
    e = lax.axis_index("expert")
    p = lax.axis_index("pipe")
    h = e // SHARING_CARDS
    m = e % SHARING_CARDS
    base = h * SHARING_CARDS
    c = m % 2
    o = 1 - c
    q = m // 2
    qx, qz = flip(q, 1), flip(q, 2)
    qd = flip(qx, 2)
    sib = {"expert": base + flip(m, 1)}
    xn = {"expert": base + flip(m, 2)}
    zn = {"expert": base + flip(m, 4)}
    mirror = {"pipe": positions - 1 - p}
    side = p // (positions // 2)
    crosses = [{"expert": ((h + k) % experts) * SHARING_CARDS + m} for k in range(experts)]

    barrier = pltpu.get_barrier_semaphore()
    others = [sib, xn, zn, mirror] + crosses[1:]
    for other in others:
        pl.semaphore_signal(barrier, inc=1, device_id=other, device_id_type=MESH)

    weight_copies = [
        pltpu.make_async_copy(wg, wgu.at[:, pl.ds(0, hidden)], weight_s.at[0]),
        pltpu.make_async_copy(wu, wgu.at[:, pl.ds(hidden, hidden)], weight_s.at[1]),
        pltpu.make_async_copy(wd_far, wd, weight_s.at[2]),
    ]
    for copy in weight_copies:
        copy.start()

    def rc(src, dst, ss, rs, dev):
        return pltpu.make_async_remote_copy(
            src_ref=src, dst_ref=dst, send_sem=ss, recv_sem=rs, device_id=dev, device_id_type=MESH
        )

    sent = []

    def send(src, dst, ss, rs, dev):
        copy = rc(src, dst, ss, rs, dev)
        copy.start()
        sent.append(copy)

    broute_row, froute_row = broute[...], froute[...]
    bw_row, broute_col, bw_col = within(broute_row)
    fw_row, froute_col, fw_col = within(froute_row)
    at_long = lax.broadcasted_iota(jnp.int32, (experts * BLOCK, tokens), 0)
    at_short = lax.broadcasted_iota(jnp.int32, (experts * PAD, tokens), 0)
    y_slots = one_hot(at_long == broute_row * BLOCK + bw_row)
    g_slots = one_hot(at_long == broute_row * BLOCK + SLOTS + bw_row)
    x_slots = one_hot((at_long == froute_row * BLOCK + 2 * SLOTS + fw_row) & (fw_row < 8))
    scaled = (row_and_column(bgate[...]) * cot[...].astype(jnp.float32)).astype(jnp.bfloat16)

    def place(half):
        at = pl.ds(half * middle, middle)
        placed_b[half] = (
            (
                matmul(y_slots, btok[:, at])
                + matmul(g_slots, scaled[:, half * middle : (half + 1) * middle])
                + matmul(x_slots, ftok[:, at])
            )
            .astype(jnp.bfloat16)
            .reshape(experts, BLOCK, middle)
        )
        all_b[half, c, q, h] = placed_b[half, h]

    def place_tail():
        tail = jnp.zeros((experts * PAD, quarter), jnp.float32)
        for part in range(4):
            slots = one_hot((at_short == froute_row * PAD + 4 * part + fw_row - 8) & (fw_row >= 8))
            tail = tail + matmul(slots, ftok[:, pl.ds(part * quarter, quarter)])
        placed_f[...] = tail.astype(jnp.bfloat16).reshape(experts, PAD, quarter)
        all_f[c, q, h] = placed_f[h]

    place(0)
    pl.semaphore_wait(barrier, len(others))

    streams = (
        (placed_b.at[0], all_b.at[0]),
        (placed_b.at[1], all_b.at[1]),
        (placed_f, all_f),
    )

    def origin(k):
        return (h + experts - k) % experts

    def cross_send(s):
        placed, alls = streams[s]
        for k in range(1, experts):
            send(
                placed.at[(h + k) % experts],
                alls.at[c, q, h],
                cross_s.at[s, k],
                cross_r.at[s, k],
                crosses[k],
            )

    def spread(s, k, kind, part, dev):
        slot = streams[s][1].at[part[0], part[1], origin(k)]
        send(slot, slot, disp_s.at[s, k, kind], disp_r.at[s, k, kind], dev)

    def arrive(s, k, kind, part, dev):
        slot = streams[s][1].at[part[0], part[1], origin(k)]
        rc(slot, slot, disp_s.at[s, k, kind], disp_r.at[s, k, kind], dev).wait_recv()

    def direct(s, k):
        if k > 0:
            slot = streams[s][1].at[c, q, origin(k)]
            rc(slot, slot, cross_s.at[s, k], cross_r.at[s, k], crosses[k]).wait_recv()
        spread(s, k, 0, (c, q), xn)
        spread(s, k, 1, (c, q), zn)
        spread(s, k, 2, (c, q), sib)

    def by_z(s, k):
        return k % 2 == 0 and s == 0

    def forward(s, k):
        arrive(s, k, 0, (c, qx), xn)
        if by_z(s, k):
            spread(s, k, 5, (c, qx), zn)
        spread(s, k, 3, (c, qx), sib)
        arrive(s, k, 1, (c, qz), zn)
        if not by_z(s, k):
            spread(s, k, 5, (c, qz), xn)
        spread(s, k, 4, (c, qz), sib)

    def last(s, k):
        arrive(s, k, 5, (c, qd), zn if by_z(s, k) else xn)
        spread(s, k, 6, (c, qd), sib)

    def complete(s, k):
        arrive(s, k, 2, (o, q), sib)
        arrive(s, k, 3, (o, qx), sib)
        arrive(s, k, 4, (o, qz), sib)
        arrive(s, k, 6, (o, qd), sib)

    quarters = (q, qx, qz, qd)

    def mirror_copy(k, at):
        j, own = origin(k), quarters[at]
        return (
            all_b.at[1 - side, c, own, j],
            mirrored.at[c, own, j],
            pipe_s.at[k, at],
            pipe_r.at[k, at],
            mirror,
        )

    def mirror_send(k, at):
        send(*mirror_copy(k, at))

    def mirror_arrive(k, at):
        rc(*mirror_copy(k, at)).wait_recv()
        slot = mirrored.at[c, quarters[at], origin(k)]
        send(slot, slot, side_s.at[k, at], side_r.at[k, at], sib)

    def mirror_complete(k, at):
        slot = mirrored.at[o, quarters[at], origin(k)]
        rc(slot, slot, side_s.at[k, at], side_r.at[k, at], sib).wait_recv()

    def columns(i):
        return pl.ds(pl.multiple_of(i * chunk, chunk), chunk)

    def far_columns(start, i):
        return pl.ds(pl.multiple_of(start + i * chunk, chunk), chunk)

    def first_products(k, half):
        j = origin(k)

        def step(i, carry):
            at = far_columns(half * middle, i)
            block = all_b[half, :, :, j, :, columns(i)].reshape(SHARING_CARDS * BLOCK, chunk)
            both = matmul(block, wgu[at, :]).reshape(SHARING_CARDS, BLOCK, 2 * hidden)
            down = contract_last(block, wd[:, at]).reshape(SHARING_CARDS, BLOCK, hidden)
            pre[:, j] += both
            hgrad[:, j] += down
            return carry

        lax.fori_loop(0, steps, step, 0)

    later = range(1, experts)
    cross_send(0)
    direct(0, 0)
    place(1)
    cross_send(1)
    direct(1, 0)
    place_tail()
    cross_send(2)
    direct(2, 0)
    mirror_send(0, 0)
    pre[...] = jnp.zeros_like(pre)
    hgrad[...] = jnp.zeros_like(hgrad)
    forward(0, 0)
    forward(1, 0)
    mirror_send(0, 1)
    mirror_send(0, 2)
    for k in later:
        direct(0, k)
    last(0, 0)
    last(1, 0)
    mirror_send(0, 3)
    forward(2, 0)
    for k in later:
        direct(1, k)
        mirror_send(k, 0)
        direct(2, k)
    last(2, 0)
    for copy in weight_copies:
        copy.wait()
    complete(0, 0)
    first_products(0, 0)
    for k in later:
        forward(0, k)
    complete(1, 0)
    first_products(0, 1)
    for k in later:
        forward(1, k)
        mirror_send(k, 1)
        mirror_send(k, 2)
        forward(2, k)
    for k in later:
        for s in range(3):
            last(s, k)
        mirror_send(k, 3)
    for k in later:
        complete(0, k)
        first_products(k, 0)
    for k in later:
        complete(1, k)
        first_products(k, 1)
    for k in range(experts):
        complete(2, k)

    def part_of(value, start):
        return value.reshape(blocks, BLOCK, value.shape[1])[:, start : start + PAD].reshape(
            rows, value.shape[1]
        )

    in_block = lax.broadcasted_iota(jnp.int32, (rows, 1), 0) % PAD
    valid = in_block < SLOTS
    pre_all = pre[...].reshape(long_rows, 2 * hidden)
    hgrad_all = hgrad[...].reshape(long_rows, hidden)
    pre_y = part_of(pre_all, 0)
    gate_pre, up_pre = pre_y[:, :hidden], pre_y[:, hidden:]
    hidden_grad = part_of(pltpu.roll(hgrad_all, long_rows - SLOTS, 0), 0)
    sigma = 1.0 / (1.0 + jnp.exp(-gate_pre))
    activated = gate_pre * sigma
    grads[:, 2 * hidden :] = jnp.where(valid, activated * up_pre, 0.0).astype(jnp.bfloat16)
    grads[:, :hidden] = jnp.where(
        valid, hidden_grad * up_pre * sigma * (1.0 + gate_pre * (1.0 - sigma)), 0.0
    ).astype(jnp.bfloat16)
    grads[:, hidden : 2 * hidden] = jnp.where(valid, hidden_grad * activated, 0.0).astype(
        jnp.bfloat16
    )
    send(grads, mgrads, pipe_s.at[0, 4], pipe_r.at[0, 4], mirror)

    def silu_product(value):
        gate, up = value[:, :hidden], value[:, hidden:]
        return gate / (1.0 + jnp.exp(-gate)) * up

    short = all_f[...].reshape(rows, quarter)
    pre_f = matmul(short, wgu[pl.ds(0, quarter), :])
    for part in range(1, 4):
        partial = matmul(short, wgu[pl.ds(part * quarter, quarter), :])
        pre_f = pre_f + pltpu.roll(partial, rows - 4 * part, 0)
    left1[...] = jnp.where(valid, 0.0, pltpu.roll(silu_product(pre_f), SLOTS, 0)).astype(
        jnp.bfloat16
    )
    hid8 = silu_product(part_of(pre_all, PAD))
    left2[:, :hidden] = jnp.where(in_block < 8, pltpu.roll(hid8, rows - 8, 0), 0.0).astype(
        jnp.bfloat16
    )
    left2[:, hidden:] = jnp.where(in_block < 8, 0.0, hid8).astype(jnp.bfloat16)

    def make_parts(s):
        def step(i, carry):
            at = columns(i)
            if s < 2:
                far = far_columns(s * middle, i)
                value = contract_last(grads[:, : 2 * hidden], wgu[far, :])
                value = value + matmul(left1[...], wd[:, far])
            else:
                value = matmul(left2[:, :hidden], wd[:, at])
                value = value + matmul(left2[:, hidden:], wd[:, far_columns(middle, i)])
            parts[s, :, :, :, :, at] = value.astype(jnp.bfloat16).reshape(
                2, 4, experts, PAD, chunk
            )
            return carry

        lax.fori_loop(0, steps, step, 0)
        send(parts.at[s, o], r1.at[s], ret_s.at[s, 0], ret_r.at[s, 0], sib)

    def x_first(s, j):
        return j % 2 == 0 or s > 0

    def pass_copy(s, j):
        return (
            parts.at[s, c, qd, j],
            r2a.at[s, j],
            back_s.at[s, j, 0],
            back_r.at[s, j, 0],
            xn if x_first(s, j) else zn,
        )

    def x_copy(s, j):
        return parts.at[s, c, qx, j], r2x.at[s, j], back_s.at[s, j, 1], back_r.at[s, j, 1], xn

    def z_copy(s, j):
        return parts.at[s, c, qz, j], r2z.at[s, j], back_s.at[s, j, 2], back_r.at[s, j, 2], zn

    def pair_sum(s):
        rc(parts.at[s, o], r1.at[s], ret_s.at[s, 0], ret_r.at[s, 0], sib).wait_recv()

        def add(first):
            parts[s, c, first] = (
                parts[s, c, first].astype(jnp.float32) + r1[s, first].astype(jnp.float32)
            ).astype(jnp.bfloat16)

        add(qd)
        for j in range(experts):
            send(*pass_copy(s, j))
        add(qx)
        for j in range(experts):
            if x_first(s, j):
                send(*x_copy(s, j))
        add(qz)
        for j in range(experts):
            if not x_first(s, j):
                send(*z_copy(s, j))
        add(q)

    def passed_on(s):
        for j in range(experts):
            rc(*pass_copy(s, j)).wait_recv()
            to = qz if x_first(s, j) else qx
            parts[s, c, to, j] = (
                parts[s, c, to, j].astype(jnp.float32) + r2a[s, j].astype(jnp.float32)
            ).astype(jnp.bfloat16)
            if x_first(s, j):
                send(*z_copy(s, j))
            else:
                send(*x_copy(s, j))

    def summed(s):
        for j in range(experts):
            rc(*x_copy(s, j)).wait_recv()
            rc(*z_copy(s, j)).wait_recv()
            tsend[s, j] = (
                parts[s, c, q, j].astype(jnp.float32)
                + r2x[s, j].astype(jnp.float32)
                + r2z[s, j].astype(jnp.float32)
            ).astype(jnp.bfloat16)
        for k in later:
            send(
                tsend.at[s, (h + k) % experts],
                r3.at[s, h],
                ret_s.at[s, k],
                ret_r.at[s, k],
                crosses[k],
            )
        r3[s, h] = tsend[s, h]

    def home(s):
        for k in later:
            slot = r3.at[s, origin(k)]
            rc(slot, slot, ret_s.at[s, k], ret_r.at[s, k], crosses[k]).wait_recv()
        return r3[s].reshape(experts * PAD, middle)

    def transposed(source, target):
        spaced[:, :PAD] = source[...].reshape(blocks, PAD, 3 * hidden)
        spaced[:, PAD:] = jnp.zeros((blocks, BLOCK - PAD, 3 * hidden), jnp.bfloat16)
        full = spaced[...].reshape(long_rows, 3 * hidden)
        target[: 2 * hidden, :] = full[:, : 2 * hidden].T
        down = pltpu.roll(full[:, 2 * hidden :].astype(jnp.float32), SLOTS, 0)
        target[2 * hidden :, :] = down.astype(jnp.bfloat16).T

    def weight_grads(first, end):
        def step(i, carry):
            at = columns(i)
            block = all_b[side, :, :, :, :, at].reshape(long_rows, chunk)
            far = mirrored[:, :, :, :, at].reshape(long_rows, chunk)
            total = matmul(grads_t[...], block) + matmul(mgrads_t[...], far)
            both = total[: 2 * hidden].T.astype(jnp.bfloat16)
            out_g[at, :] = both[:, :hidden]
            out_u[at, :] = both[:, hidden:]
            out_d[:, at] = total[2 * hidden :].astype(jnp.bfloat16)
            return carry

        lax.fori_loop(first, end, step, 0)

    make_parts(0)
    make_parts(1)
    pair_sum(0)
    make_parts(2)
    pair_sum(1)
    for k in range(experts):
        for at in range(4):
            mirror_arrive(k, at)
    passed_on(0)
    pair_sum(2)
    transposed(grads, grads_t)
    passed_on(1)
    rc(grads, mgrads, pipe_s.at[0, 4], pipe_r.at[0, 4], mirror).wait_recv()
    transposed(mgrads, mgrads_t)
    for k in range(experts):
        for at in range(4):
            mirror_complete(k, at)
    summed(0)
    passed_on(2)
    weight_grads(0, steps // 3)
    summed(1)
    weight_grads(steps // 3, 2 * steps // 3)
    summed(2)
    weight_grads(2 * steps // 3, steps)
    results = [
        pltpu.make_async_copy(out_g, far_g, out_s.at[0]),
        pltpu.make_async_copy(out_u, far_u, out_s.at[1]),
        pltpu.make_async_copy(out_d, far_d, out_s.at[2]),
    ]
    for copy in results:
        copy.start()

    at_t = lax.broadcasted_iota(jnp.int32, (tokens, experts * PAD), 1)
    b_slots = one_hot(at_t == broute_col * PAD + bw_col)
    f_last = one_hot((at_t == froute_col * PAD + fw_col + 4) & (fw_col >= 8))
    f_left = one_hot((at_t == froute_col * PAD + fw_col) & (fw_col < 8))
    f_right = one_hot((at_t == froute_col * PAD + fw_col + 8) & (fw_col < 8))
    fgate_col = row_and_column(fgate[...])
    first = home(0)
    out_b[:, :middle] = matmul(b_slots, first).astype(jnp.bfloat16)
    second = home(1)
    out_b[:, middle:] = matmul(b_slots, second).astype(jnp.bfloat16)
    third = home(2)
    out_f[:, :middle] = (fgate_col * (matmul(f_last, first) + matmul(f_left, third))).astype(
        jnp.bfloat16
    )
    out_f[:, middle:] = (fgate_col * (matmul(f_last, second) + matmul(f_right, third))).astype(
        jnp.bfloat16
    )
    for copy in results:
        copy.wait()
    for copy in sent:
        copy.wait_send()


def hand_out(*refs):
    sources, targets, held, sems = refs[:5], refs[5:10], refs[10:15], refs[15]
    reads = [pltpu.make_async_copy(sources[i], held[i], sems.at[0, i]) for i in range(5)]
    writes = [pltpu.make_async_copy(held[i], targets[i], sems.at[1, i]) for i in range(5)]
    for read in reads:
        read.start()
    for read, write in zip(reads, writes):
        read.wait()
        write.start()
    for write in writes:
        write.wait()


def on_device(
    forward_tokens,
    forward_routing,
    forward_gates,
    backward_tokens,
    backward_routing,
    backward_gates,
    cotangent,
    gate_matrix,
    up_matrix,
    down_matrix,
):
    devices = lax.axis_size("expert")
    positions = lax.axis_size("pipe")
    experts = devices // SHARING_CARDS
    tokens, width = forward_tokens.shape[1:]
    hidden = gate_matrix.shape[2]
    middle = width // 2
    blocks = SHARING_CARDS * experts
    rows = blocks * PAD
    assert max(tokens // 3, tokens // experts) <= SLOTS
    bf16, f32 = jnp.bfloat16, jnp.float32
    vmem = pl.BlockSpec(memory_space=pltpu.VMEM)
    far = pl.BlockSpec(memory_space=pl.ANY)
    dma = pltpu.SemaphoreType.DMA
    outs = pl.pallas_call(
        functools.partial(kernel, experts, positions),
        out_shape=(
            jax.ShapeDtypeStruct((tokens, width), bf16),
            jax.ShapeDtypeStruct((tokens, width), bf16),
            jax.ShapeDtypeStruct((middle, hidden), bf16),
            jax.ShapeDtypeStruct((middle, hidden), bf16),
            jax.ShapeDtypeStruct((hidden, middle), bf16),
        ),
        in_specs=[vmem] * 7 + [far] * 3,
        out_specs=(vmem,) * 2 + (far,) * 3,
        scratch_shapes=[
            pltpu.VMEM((middle, hidden), bf16),
            pltpu.VMEM((middle, hidden), bf16),
            pltpu.VMEM((hidden, middle), bf16),
            pltpu.VMEM((width, 2 * hidden), bf16),
            pltpu.VMEM((hidden, width), bf16),
            pltpu.VMEM((2, experts, BLOCK, middle), bf16),
            pltpu.VMEM((experts, PAD, width // 4), bf16),
            pltpu.VMEM((2, 2, 4, experts, BLOCK, middle), bf16),
            pltpu.VMEM((2, 4, experts, PAD, width // 4), bf16),
            pltpu.VMEM((3, 2, 4, experts, PAD, middle), bf16),
            pltpu.VMEM((3, 4, experts, PAD, middle), bf16),
            pltpu.VMEM((3, experts, PAD, middle), bf16),
            pltpu.VMEM((3, experts, PAD, middle), bf16),
            pltpu.VMEM((3, experts, PAD, middle), bf16),
            pltpu.VMEM((3, experts, PAD, middle), bf16),
            pltpu.VMEM((3, experts, PAD, middle), bf16),
            pltpu.VMEM((SHARING_CARDS, experts, BLOCK, 2 * hidden), f32),
            pltpu.VMEM((SHARING_CARDS, experts, BLOCK, hidden), f32),
            pltpu.VMEM((rows, 3 * hidden), bf16),
            pltpu.VMEM((rows, 3 * hidden), bf16),
            pltpu.VMEM((blocks, BLOCK, 3 * hidden), bf16),
            pltpu.VMEM((3 * hidden, blocks * BLOCK), bf16),
            pltpu.VMEM((3 * hidden, blocks * BLOCK), bf16),
            pltpu.VMEM((rows, hidden), bf16),
            pltpu.VMEM((rows, 2 * hidden), bf16),
            pltpu.VMEM((2, 4, experts, BLOCK, middle), bf16),
            dma((3,)),
            dma((3,)),
            dma((3, experts)),
            dma((3, experts)),
            dma((3, experts, 7)),
            dma((3, experts, 7)),
            dma((3, experts)),
            dma((3, experts)),
            dma((3, experts, 3)),
            dma((3, experts, 3)),
            dma((experts, 5)),
            dma((experts, 5)),
            dma((experts, 4)),
            dma((experts, 4)),
        ],
        compiler_params=pltpu.CompilerParams(
            collective_id=0, has_side_effects=True, vmem_limit_bytes=60 * 1024 * 1024
        ),
    )(
        forward_tokens[0],
        forward_routing.reshape(1, tokens),
        forward_gates,
        backward_tokens[0],
        backward_routing.reshape(1, tokens),
        backward_gates,
        cotangent[0],
        gate_matrix[0],
        up_matrix[0],
        down_matrix[0],
    )
    outs = pl.pallas_call(
        hand_out,
        out_shape=tuple(jax.ShapeDtypeStruct(out.shape, bf16) for out in outs),
        in_specs=[pl.BlockSpec(memory_space=pl.ANY)] * 5,
        out_specs=(pl.BlockSpec(memory_space=pl.ANY),) * 5,
        scratch_shapes=[pltpu.VMEM(out.shape, bf16) for out in outs] + [dma((2, 5))],
        compiler_params=pltpu.CompilerParams(vmem_limit_bytes=60 * 1024 * 1024),
    )(*outs)
    return tuple(out[None] for out in outs)


def solution(mesh):
    in_specs = (
        P("pipe", "expert", None),
        P("pipe", "expert", None),
        P("pipe", "expert"),
        P("pipe", "expert", None),
        P("pipe", "expert", None),
        P("pipe", "expert"),
        P("pipe", "expert", None),
        P("pipe", None, "expert"),
        P("pipe", None, "expert"),
        P("pipe", "expert", None),
    )
    out_specs = (
        P("pipe", "expert", None),
        P("pipe", "expert", None),
        P("pipe", None, "expert"),
        P("pipe", None, "expert"),
        P("pipe", "expert", None),
    )
    return jax.shard_map(
        on_device, mesh=mesh, in_specs=in_specs, out_specs=out_specs, check_vma=False
    )
```

```python
import functools

import jax
import jax.numpy as jnp
from jax import lax
from jax.experimental import pallas as pl
from jax.experimental.pallas import tpu as pltpu
from jax.sharding import PartitionSpec as P

SHARING_CARDS = 8
PAD = 16
SLOTS = 12
BLOCK = 32
MESH = pl.DeviceIdType.MESH


def flip(value, bit):
    return value + bit - 2 * bit * ((value // bit) % 2)


def contract_last(left, right):
    return lax.dot_general(
        left, right, (((1,), (1,)), ((), ())), preferred_element_type=jnp.float32
    )


def matmul(left, right):
    return jnp.dot(left, right, preferred_element_type=jnp.float32)


def row_and_column(row):
    n = row.shape[1]
    at0 = lax.broadcasted_iota(jnp.int32, (n, n), 0)
    at1 = lax.broadcasted_iota(jnp.int32, (n, n), 1)
    return jnp.sum(jnp.where(at0 == at1, row, jnp.zeros_like(row)), axis=1, keepdims=True)


def within(routing_row):
    n = routing_row.shape[1]
    column = row_and_column(routing_row)
    at0 = lax.broadcasted_iota(jnp.int32, (n, n), 0)
    at1 = lax.broadcasted_iota(jnp.int32, (n, n), 1)
    same = column == routing_row
    before_row = jnp.sum(jnp.where(same & (at0 < at1), 1.0, 0.0), axis=0, keepdims=True)
    before_column = jnp.sum(jnp.where(same & (at1 < at0), 1.0, 0.0), axis=1, keepdims=True)
    return before_row.astype(jnp.int32), column, before_column.astype(jnp.int32)


def one_hot(condition):
    return jnp.where(condition, 1.0, 0.0).astype(jnp.bfloat16)


def kernel(
    experts,
    positions,
    ftok,
    froute,
    fgate,
    btok,
    broute,
    bgate,
    cot,
    wg,
    wu,
    wd_far,
    out_f,
    out_b,
    out_g,
    out_u,
    out_d,
    wgu,
    wd,
    placed_b,
    placed_f,
    all_b,
    all_f,
    parts,
    r1,
    r2a,
    r2x,
    r2z,
    tsend,
    r3,
    pre,
    hgrad,
    grads,
    mgrads,
    spaced,
    grads_t,
    mgrads_t,
    left1,
    left2,
    mirrored,
    weight_s,
    cross_s,
    cross_r,
    disp_s,
    disp_r,
    ret_s,
    ret_r,
    back_s,
    back_r,
    pipe_s,
    pipe_r,
    side_s,
    side_r,
):
    tokens, width = ftok.shape
    hidden = wg.shape[1]
    middle = width // 2
    quarter = width // 4
    chunk = 896
    steps = middle // chunk
    blocks = SHARING_CARDS * experts
    rows = blocks * PAD
    long_rows = blocks * BLOCK
    e = lax.axis_index("expert")
    p = lax.axis_index("pipe")
    h = e // SHARING_CARDS
    m = e % SHARING_CARDS
    base = h * SHARING_CARDS
    c = m % 2
    o = 1 - c
    q = m // 2
    qx, qz = flip(q, 1), flip(q, 2)
    qd = flip(qx, 2)
    sib = {"expert": base + flip(m, 1)}
    xn = {"expert": base + flip(m, 2)}
    zn = {"expert": base + flip(m, 4)}
    mirror = {"pipe": positions - 1 - p}
    side = p // (positions // 2)
    crosses = [{"expert": ((h + k) % experts) * SHARING_CARDS + m} for k in range(experts)]

    barrier = pltpu.get_barrier_semaphore()
    others = [sib, xn, zn, mirror] + crosses[1:]
    for other in others:
        pl.semaphore_signal(barrier, inc=1, device_id=other, device_id_type=MESH)

    weight_copies = [
        pltpu.make_async_copy(wg, wgu.at[:, pl.ds(0, hidden)], weight_s.at[0]),
        pltpu.make_async_copy(wu, wgu.at[:, pl.ds(hidden, hidden)], weight_s.at[1]),
        pltpu.make_async_copy(wd_far, wd, weight_s.at[2]),
    ]
    for copy in weight_copies:
        copy.start()

    def rc(src, dst, ss, rs, dev):
        return pltpu.make_async_remote_copy(
            src_ref=src, dst_ref=dst, send_sem=ss, recv_sem=rs, device_id=dev, device_id_type=MESH
        )

    sent = []

    def send(src, dst, ss, rs, dev):
        copy = rc(src, dst, ss, rs, dev)
        copy.start()
        sent.append(copy)

    broute_row, froute_row = broute[...], froute[...]
    bw_row, broute_col, bw_col = within(broute_row)
    fw_row, froute_col, fw_col = within(froute_row)
    at_long = lax.broadcasted_iota(jnp.int32, (experts * BLOCK, tokens), 0)
    at_short = lax.broadcasted_iota(jnp.int32, (experts * PAD, tokens), 0)
    y_slots = one_hot(at_long == broute_row * BLOCK + bw_row)
    g_slots = one_hot(at_long == broute_row * BLOCK + SLOTS + bw_row)
    x_slots = one_hot((at_long == froute_row * BLOCK + 2 * SLOTS + fw_row) & (fw_row < 8))
    scaled = (row_and_column(bgate[...]) * cot[...].astype(jnp.float32)).astype(jnp.bfloat16)
    for half in range(2):
        at = pl.ds(half * middle, middle)
        placed_b[half] = (
            (
                matmul(y_slots, btok[:, at])
                + matmul(g_slots, scaled[:, half * middle : (half + 1) * middle])
                + matmul(x_slots, ftok[:, at])
            )
            .astype(jnp.bfloat16)
            .reshape(experts, BLOCK, middle)
        )
        all_b[half, c, q, h] = placed_b[half, h]
    tail = jnp.zeros((experts * PAD, quarter), jnp.float32)
    for part in range(4):
        slots = one_hot((at_short == froute_row * PAD + 4 * part + fw_row - 8) & (fw_row >= 8))
        tail = tail + matmul(slots, ftok[:, pl.ds(part * quarter, quarter)])
    placed_f[...] = tail.astype(jnp.bfloat16).reshape(experts, PAD, quarter)
    all_f[c, q, h] = placed_f[h]

    pl.semaphore_wait(barrier, len(others))

    streams = (
        (placed_b.at[0], all_b.at[0]),
        (placed_b.at[1], all_b.at[1]),
        (placed_f, all_f),
    )

    def origin(k):
        return (h + experts - k) % experts

    def cross_send(s):
        placed, alls = streams[s]
        for k in range(1, experts):
            send(
                placed.at[(h + k) % experts],
                alls.at[c, q, h],
                cross_s.at[s, k],
                cross_r.at[s, k],
                crosses[k],
            )

    def spread(s, k, kind, part, dev):
        slot = streams[s][1].at[part[0], part[1], origin(k)]
        send(slot, slot, disp_s.at[s, k, kind], disp_r.at[s, k, kind], dev)

    def arrive(s, k, kind, part, dev):
        slot = streams[s][1].at[part[0], part[1], origin(k)]
        rc(slot, slot, disp_s.at[s, k, kind], disp_r.at[s, k, kind], dev).wait_recv()

    def direct(s, k):
        if k > 0:
            slot = streams[s][1].at[c, q, origin(k)]
            rc(slot, slot, cross_s.at[s, k], cross_r.at[s, k], crosses[k]).wait_recv()
        spread(s, k, 0, (c, q), xn)
        spread(s, k, 1, (c, q), zn)
        spread(s, k, 2, (c, q), sib)

    def by_z(s, k):
        return k % 2 == 0 and s == 0

    def forward(s, k):
        arrive(s, k, 0, (c, qx), xn)
        if by_z(s, k):
            spread(s, k, 5, (c, qx), zn)
        spread(s, k, 3, (c, qx), sib)
        arrive(s, k, 1, (c, qz), zn)
        if not by_z(s, k):
            spread(s, k, 5, (c, qz), xn)
        spread(s, k, 4, (c, qz), sib)

    def last(s, k):
        arrive(s, k, 5, (c, qd), zn if by_z(s, k) else xn)
        spread(s, k, 6, (c, qd), sib)

    def complete(s, k):
        arrive(s, k, 2, (o, q), sib)
        arrive(s, k, 3, (o, qx), sib)
        arrive(s, k, 4, (o, qz), sib)
        arrive(s, k, 6, (o, qd), sib)

    quarters = (q, qx, qz, qd)

    def mirror_copy(k, at):
        j, own = origin(k), quarters[at]
        return (
            all_b.at[1 - side, c, own, j],
            mirrored.at[c, own, j],
            pipe_s.at[k, at],
            pipe_r.at[k, at],
            mirror,
        )

    def mirror_send(k, at):
        send(*mirror_copy(k, at))

    def mirror_arrive(k, at):
        rc(*mirror_copy(k, at)).wait_recv()
        slot = mirrored.at[c, quarters[at], origin(k)]
        send(slot, slot, side_s.at[k, at], side_r.at[k, at], sib)

    def mirror_complete(k, at):
        slot = mirrored.at[o, quarters[at], origin(k)]
        rc(slot, slot, side_s.at[k, at], side_r.at[k, at], sib).wait_recv()

    def columns(i):
        return pl.ds(pl.multiple_of(i * chunk, chunk), chunk)

    def far_columns(start, i):
        return pl.ds(pl.multiple_of(start + i * chunk, chunk), chunk)

    def first_products(k, half):
        j = origin(k)

        def step(i, carry):
            at = far_columns(half * middle, i)
            block = all_b[half, :, :, j, :, columns(i)].reshape(SHARING_CARDS * BLOCK, chunk)
            both = matmul(block, wgu[at, :]).reshape(SHARING_CARDS, BLOCK, 2 * hidden)
            down = contract_last(block, wd[:, at]).reshape(SHARING_CARDS, BLOCK, hidden)
            pre[:, j] += both
            hgrad[:, j] += down
            return carry

        lax.fori_loop(0, steps, step, 0)

    later = range(1, experts)
    for s in range(3):
        cross_send(s)
        direct(s, 0)
    mirror_send(0, 0)
    pre[...] = jnp.zeros_like(pre)
    hgrad[...] = jnp.zeros_like(hgrad)
    forward(0, 0)
    forward(1, 0)
    mirror_send(0, 1)
    mirror_send(0, 2)
    for k in later:
        direct(0, k)
    last(0, 0)
    last(1, 0)
    mirror_send(0, 3)
    forward(2, 0)
    for k in later:
        direct(1, k)
        mirror_send(k, 0)
        direct(2, k)
    last(2, 0)
    for copy in weight_copies:
        copy.wait()
    complete(0, 0)
    first_products(0, 0)
    for k in later:
        forward(0, k)
    complete(1, 0)
    first_products(0, 1)
    for k in later:
        forward(1, k)
        mirror_send(k, 1)
        mirror_send(k, 2)
        forward(2, k)
    for k in later:
        for s in range(3):
            last(s, k)
        mirror_send(k, 3)
    for k in later:
        complete(0, k)
        first_products(k, 0)
    for k in later:
        complete(1, k)
        first_products(k, 1)
    for k in range(experts):
        complete(2, k)

    def part_of(value, start):
        return value.reshape(blocks, BLOCK, value.shape[1])[:, start : start + PAD].reshape(
            rows, value.shape[1]
        )

    in_block = lax.broadcasted_iota(jnp.int32, (rows, 1), 0) % PAD
    valid = in_block < SLOTS
    pre_all = pre[...].reshape(long_rows, 2 * hidden)
    hgrad_all = hgrad[...].reshape(long_rows, hidden)
    pre_y = part_of(pre_all, 0)
    gate_pre, up_pre = pre_y[:, :hidden], pre_y[:, hidden:]
    hidden_grad = part_of(pltpu.roll(hgrad_all, long_rows - SLOTS, 0), 0)
    sigma = 1.0 / (1.0 + jnp.exp(-gate_pre))
    activated = gate_pre * sigma
    grads[:, 2 * hidden :] = jnp.where(valid, activated * up_pre, 0.0).astype(jnp.bfloat16)
    grads[:, :hidden] = jnp.where(
        valid, hidden_grad * up_pre * sigma * (1.0 + gate_pre * (1.0 - sigma)), 0.0
    ).astype(jnp.bfloat16)
    grads[:, hidden : 2 * hidden] = jnp.where(valid, hidden_grad * activated, 0.0).astype(
        jnp.bfloat16
    )
    send(grads, mgrads, pipe_s.at[0, 4], pipe_r.at[0, 4], mirror)

    def silu_product(value):
        gate, up = value[:, :hidden], value[:, hidden:]
        return gate / (1.0 + jnp.exp(-gate)) * up

    short = all_f[...].reshape(rows, quarter)
    pre_f = matmul(short, wgu[pl.ds(0, quarter), :])
    for part in range(1, 4):
        partial = matmul(short, wgu[pl.ds(part * quarter, quarter), :])
        pre_f = pre_f + pltpu.roll(partial, rows - 4 * part, 0)
    left1[...] = jnp.where(valid, 0.0, pltpu.roll(silu_product(pre_f), SLOTS, 0)).astype(
        jnp.bfloat16
    )
    hid8 = silu_product(part_of(pre_all, PAD))
    left2[:, :hidden] = jnp.where(in_block < 8, pltpu.roll(hid8, rows - 8, 0), 0.0).astype(
        jnp.bfloat16
    )
    left2[:, hidden:] = jnp.where(in_block < 8, 0.0, hid8).astype(jnp.bfloat16)

    def make_parts(s):
        def step(i, carry):
            at = columns(i)
            if s < 2:
                far = far_columns(s * middle, i)
                value = contract_last(grads[:, : 2 * hidden], wgu[far, :])
                value = value + matmul(left1[...], wd[:, far])
            else:
                value = matmul(left2[:, :hidden], wd[:, at])
                value = value + matmul(left2[:, hidden:], wd[:, far_columns(middle, i)])
            parts[s, :, :, :, :, at] = value.astype(jnp.bfloat16).reshape(
                2, 4, experts, PAD, chunk
            )
            return carry

        lax.fori_loop(0, steps, step, 0)
        send(parts.at[s, o], r1.at[s], ret_s.at[s, 0], ret_r.at[s, 0], sib)

    def x_first(s, j):
        return j % 2 == 0 or s > 0

    def pass_copy(s, j):
        return (
            parts.at[s, c, qd, j],
            r2a.at[s, j],
            back_s.at[s, j, 0],
            back_r.at[s, j, 0],
            xn if x_first(s, j) else zn,
        )

    def x_copy(s, j):
        return parts.at[s, c, qx, j], r2x.at[s, j], back_s.at[s, j, 1], back_r.at[s, j, 1], xn

    def z_copy(s, j):
        return parts.at[s, c, qz, j], r2z.at[s, j], back_s.at[s, j, 2], back_r.at[s, j, 2], zn

    def pair_sum(s):
        rc(parts.at[s, o], r1.at[s], ret_s.at[s, 0], ret_r.at[s, 0], sib).wait_recv()

        def add(first):
            parts[s, c, first] = (
                parts[s, c, first].astype(jnp.float32) + r1[s, first].astype(jnp.float32)
            ).astype(jnp.bfloat16)

        add(qd)
        for j in range(experts):
            send(*pass_copy(s, j))
        add(qx)
        for j in range(experts):
            if x_first(s, j):
                send(*x_copy(s, j))
        add(qz)
        for j in range(experts):
            if not x_first(s, j):
                send(*z_copy(s, j))
        add(q)

    def passed_on(s):
        for j in range(experts):
            rc(*pass_copy(s, j)).wait_recv()
            to = qz if x_first(s, j) else qx
            parts[s, c, to, j] = (
                parts[s, c, to, j].astype(jnp.float32) + r2a[s, j].astype(jnp.float32)
            ).astype(jnp.bfloat16)
            if x_first(s, j):
                send(*z_copy(s, j))
            else:
                send(*x_copy(s, j))

    def summed(s):
        for j in range(experts):
            rc(*x_copy(s, j)).wait_recv()
            rc(*z_copy(s, j)).wait_recv()
            tsend[s, j] = (
                parts[s, c, q, j].astype(jnp.float32)
                + r2x[s, j].astype(jnp.float32)
                + r2z[s, j].astype(jnp.float32)
            ).astype(jnp.bfloat16)
        for k in later:
            send(
                tsend.at[s, (h + k) % experts],
                r3.at[s, h],
                ret_s.at[s, k],
                ret_r.at[s, k],
                crosses[k],
            )
        r3[s, h] = tsend[s, h]

    def home(s):
        for k in later:
            slot = r3.at[s, origin(k)]
            rc(slot, slot, ret_s.at[s, k], ret_r.at[s, k], crosses[k]).wait_recv()
        return r3[s].reshape(experts * PAD, middle)

    def transposed(source, target):
        spaced[:, :PAD] = source[...].reshape(blocks, PAD, 3 * hidden)
        spaced[:, PAD:] = jnp.zeros((blocks, BLOCK - PAD, 3 * hidden), jnp.bfloat16)
        full = spaced[...].reshape(long_rows, 3 * hidden)
        target[: 2 * hidden, :] = full[:, : 2 * hidden].T
        down = pltpu.roll(full[:, 2 * hidden :].astype(jnp.float32), SLOTS, 0)
        target[2 * hidden :, :] = down.astype(jnp.bfloat16).T

    def weight_grads(first, end):
        def step(i, carry):
            at = columns(i)
            block = all_b[side, :, :, :, :, at].reshape(long_rows, chunk)
            far = mirrored[:, :, :, :, at].reshape(long_rows, chunk)
            total = matmul(grads_t[...], block) + matmul(mgrads_t[...], far)
            both = total[: 2 * hidden].T.astype(jnp.bfloat16)
            out_g[at, :] = both[:, :hidden]
            out_u[at, :] = both[:, hidden:]
            out_d[:, at] = total[2 * hidden :].astype(jnp.bfloat16)
            return carry

        lax.fori_loop(first, end, step, 0)

    make_parts(0)
    make_parts(1)
    pair_sum(0)
    make_parts(2)
    pair_sum(1)
    for k in range(experts):
        for at in range(4):
            mirror_arrive(k, at)
    passed_on(0)
    pair_sum(2)
    transposed(grads, grads_t)
    passed_on(1)
    rc(grads, mgrads, pipe_s.at[0, 4], pipe_r.at[0, 4], mirror).wait_recv()
    transposed(mgrads, mgrads_t)
    for k in range(experts):
        for at in range(4):
            mirror_complete(k, at)
    summed(0)
    passed_on(2)
    weight_grads(0, steps // 3)
    summed(1)
    weight_grads(steps // 3, 2 * steps // 3)
    summed(2)
    weight_grads(2 * steps // 3, steps)

    at_t = lax.broadcasted_iota(jnp.int32, (tokens, experts * PAD), 1)
    b_slots = one_hot(at_t == broute_col * PAD + bw_col)
    f_last = one_hot((at_t == froute_col * PAD + fw_col + 4) & (fw_col >= 8))
    f_left = one_hot((at_t == froute_col * PAD + fw_col) & (fw_col < 8))
    f_right = one_hot((at_t == froute_col * PAD + fw_col + 8) & (fw_col < 8))
    fgate_col = row_and_column(fgate[...])
    first = home(0)
    out_b[:, :middle] = matmul(b_slots, first).astype(jnp.bfloat16)
    second = home(1)
    out_b[:, middle:] = matmul(b_slots, second).astype(jnp.bfloat16)
    third = home(2)
    out_f[:, :middle] = (fgate_col * (matmul(f_last, first) + matmul(f_left, third))).astype(
        jnp.bfloat16
    )
    out_f[:, middle:] = (fgate_col * (matmul(f_last, second) + matmul(f_right, third))).astype(
        jnp.bfloat16
    )
    for copy in sent:
        copy.wait_send()


def hand_out(*refs):
    sources, targets, held, sems = refs[:5], refs[5:10], refs[10:15], refs[15]
    reads = [pltpu.make_async_copy(sources[i], held[i], sems.at[0, i]) for i in range(5)]
    writes = [pltpu.make_async_copy(held[i], targets[i], sems.at[1, i]) for i in range(5)]
    for read in reads:
        read.start()
    for read, write in zip(reads, writes):
        read.wait()
        write.start()
    for write in writes:
        write.wait()


def on_device(
    forward_tokens,
    forward_routing,
    forward_gates,
    backward_tokens,
    backward_routing,
    backward_gates,
    cotangent,
    gate_matrix,
    up_matrix,
    down_matrix,
):
    devices = lax.axis_size("expert")
    positions = lax.axis_size("pipe")
    experts = devices // SHARING_CARDS
    tokens, width = forward_tokens.shape[1:]
    hidden = gate_matrix.shape[2]
    middle = width // 2
    blocks = SHARING_CARDS * experts
    rows = blocks * PAD
    assert max(tokens // 3, tokens // experts) <= SLOTS
    bf16, f32 = jnp.bfloat16, jnp.float32
    vmem = pl.BlockSpec(memory_space=pltpu.VMEM)
    far = pl.BlockSpec(memory_space=pl.ANY)
    dma = pltpu.SemaphoreType.DMA
    outs = pl.pallas_call(
        functools.partial(kernel, experts, positions),
        out_shape=(
            jax.ShapeDtypeStruct((tokens, width), bf16),
            jax.ShapeDtypeStruct((tokens, width), bf16),
            jax.ShapeDtypeStruct((middle, hidden), bf16),
            jax.ShapeDtypeStruct((middle, hidden), bf16),
            jax.ShapeDtypeStruct((hidden, middle), bf16),
        ),
        in_specs=[vmem] * 7 + [far] * 3,
        out_specs=(vmem,) * 5,
        scratch_shapes=[
            pltpu.VMEM((width, 2 * hidden), bf16),
            pltpu.VMEM((hidden, width), bf16),
            pltpu.VMEM((2, experts, BLOCK, middle), bf16),
            pltpu.VMEM((experts, PAD, width // 4), bf16),
            pltpu.VMEM((2, 2, 4, experts, BLOCK, middle), bf16),
            pltpu.VMEM((2, 4, experts, PAD, width // 4), bf16),
            pltpu.VMEM((3, 2, 4, experts, PAD, middle), bf16),
            pltpu.VMEM((3, 4, experts, PAD, middle), bf16),
            pltpu.VMEM((3, experts, PAD, middle), bf16),
            pltpu.VMEM((3, experts, PAD, middle), bf16),
            pltpu.VMEM((3, experts, PAD, middle), bf16),
            pltpu.VMEM((3, experts, PAD, middle), bf16),
            pltpu.VMEM((3, experts, PAD, middle), bf16),
            pltpu.VMEM((SHARING_CARDS, experts, BLOCK, 2 * hidden), f32),
            pltpu.VMEM((SHARING_CARDS, experts, BLOCK, hidden), f32),
            pltpu.VMEM((rows, 3 * hidden), bf16),
            pltpu.VMEM((rows, 3 * hidden), bf16),
            pltpu.VMEM((blocks, BLOCK, 3 * hidden), bf16),
            pltpu.VMEM((3 * hidden, blocks * BLOCK), bf16),
            pltpu.VMEM((3 * hidden, blocks * BLOCK), bf16),
            pltpu.VMEM((rows, hidden), bf16),
            pltpu.VMEM((rows, 2 * hidden), bf16),
            pltpu.VMEM((2, 4, experts, BLOCK, middle), bf16),
            dma((3,)),
            dma((3, experts)),
            dma((3, experts)),
            dma((3, experts, 7)),
            dma((3, experts, 7)),
            dma((3, experts)),
            dma((3, experts)),
            dma((3, experts, 3)),
            dma((3, experts, 3)),
            dma((experts, 5)),
            dma((experts, 5)),
            dma((experts, 4)),
            dma((experts, 4)),
        ],
        compiler_params=pltpu.CompilerParams(
            collective_id=0, has_side_effects=True, vmem_limit_bytes=60 * 1024 * 1024
        ),
    )(
        forward_tokens[0],
        forward_routing.reshape(1, tokens),
        forward_gates,
        backward_tokens[0],
        backward_routing.reshape(1, tokens),
        backward_gates,
        cotangent[0],
        gate_matrix[0],
        up_matrix[0],
        down_matrix[0],
    )
    outs = pl.pallas_call(
        hand_out,
        out_shape=tuple(jax.ShapeDtypeStruct(out.shape, bf16) for out in outs),
        in_specs=[pl.BlockSpec(memory_space=pl.ANY)] * 5,
        out_specs=(pl.BlockSpec(memory_space=pl.ANY),) * 5,
        scratch_shapes=[pltpu.VMEM(out.shape, bf16) for out in outs] + [dma((2, 5))],
        compiler_params=pltpu.CompilerParams(vmem_limit_bytes=60 * 1024 * 1024),
    )(*outs)
    return tuple(out[None] for out in outs)


def solution(mesh):
    in_specs = (
        P("pipe", "expert", None),
        P("pipe", "expert", None),
        P("pipe", "expert"),
        P("pipe", "expert", None),
        P("pipe", "expert", None),
        P("pipe", "expert"),
        P("pipe", "expert", None),
        P("pipe", None, "expert"),
        P("pipe", None, "expert"),
        P("pipe", "expert", None),
    )
    out_specs = (
        P("pipe", "expert", None),
        P("pipe", "expert", None),
        P("pipe", None, "expert"),
        P("pipe", None, "expert"),
        P("pipe", "expert", None),
    )
    return jax.shard_map(
        on_device, mesh=mesh, in_specs=in_specs, out_specs=out_specs, check_vma=False
    )
```
